32 devices in a mesh: span: 2 (over x), brick: 16 (over z, y, core).
Axes of the slice: x: 2, y: 2, z: 4, core: 2. Of those that a mesh axis runs over, the one named last changes fastest.
Arguments:
- measured: bfloat16 [4, 1024, 32, 128], P(None, ('span', 'brick')), parts along dimension 1, may hold values from 0.175 to 201.6, as said below
- psf: float32 [4, 3, 31], replicated, may hold values from 0.05 to 1
- stem_params: float32 [2, 16], replicated, may hold values from -4 to 4
- conv_weight: bfloat16 [432, 16], replicated, may hold values from -0.3125 to 0.3125
- head_params: float32 [2, 16], replicated, may hold values from -3 to 3
Outputs:
- estimate: float32 [1024, 32, 128], P(('span', 'brick')), parts along dimension 0
- logits: float32 [1024, 32, 128], P(('span', 'brick')), parts along dimension 0
The draws below stay inside these ranges and needn't reach their ends.
There are 2 independent parts, one for each index of `span`. The reference program is written for one: setup_inputs(seed, part) draws one part's arguments, and reference() takes and returns one part's arrays. A program takes and returns all parts, laid end to end along the dimension named above; an argument that names none is the same for every part. Nothing has to cross between parts.
Inputs may be any that keep to these rules, and one draw needn't show every extreme that they name: `measured`: positive.
All inputs are finite; a program needn't handle non-finite values.
Results may differ from the reference program's by a relative error of at most 0.0049.
Values may be sent and summed in bfloat16 or wider, within the bound.
No kernel may reach another device: no remote copies, remote signals or barrier semaphores. Data moves between devices by JAX's collectives and lax.ppermute only.
A program may use at most 128 MiB of HBM per device.

```python
import math
import jax
import jax.numpy as jnp
from jax import lax

VIEWS = 4
TAPS = 31
HALF = 15
CH = 16
ITERS = 2
CY = 32
NZ = 128
NX = 512


def draw_measured(key, part):
    signal_key, view_key = jax.random.split(key, 2)
    signal = jnp.exp(jax.random.uniform(signal_key, (1, NX, CY, NZ), jnp.float32, jnp.log(0.25), jnp.log(4.0)))
    spread = jnp.exp(jax.random.uniform(view_key, (VIEWS, NX, CY, NZ), jnp.float32, jnp.log(0.7), jnp.log(1.4)))
    depth_share = jnp.arange(NX, dtype=jnp.float32) / (NX - 1)
    fading = jnp.exp(jnp.log(3.0) * depth_share)
    values = signal * spread * fading[None, :, None, None]
    return values.astype(jnp.bfloat16)


def scatter_about(own_key, extent, deviation, most, kind=jnp.bfloat16):
    return jnp.clip(deviation * jax.random.normal(own_key, extent, jnp.float32), -most, most).astype(kind)


def setup_inputs(seed: int = 0, part: int = 0) -> dict:
    streams_of = jax.random.split(jax.random.key(seed), 6)
    part_keys = jax.random.split(jax.random.fold_in(streams_of[5], part), 6)
    return {
        "measured": draw_measured(jax.random.fold_in(jax.random.fold_in(streams_of[5], part), 71), part),
        "psf": jnp.clip(jnp.exp(jax.random.uniform(streams_of[1], (VIEWS, 3, TAPS), jnp.float32, math.log(0.05), math.log(1.0))), 0.05, 1.0),
        "stem_params": scatter_about(streams_of[2], (2, CH), 1.0, 4.0, jnp.float32),
        "conv_weight": scatter_about(streams_of[3], (27 * CH, CH), (27 * CH) ** -0.5, 0.3125),
        "head_params": scatter_about(streams_of[4], (2, CH), 0.5, 3.0, jnp.float32),
    }


HIGHEST = lax.Precision.HIGHEST


def band_matrix(kernel, row_count, col_count, offset):
    spacing = jnp.arange(col_count, dtype=jnp.int32)[None, :] - jnp.arange(row_count, dtype=jnp.int32)[:, None] + offset
    selector = (spacing[:, :, None] == jnp.arange(kernel.shape[-1], dtype=jnp.int32)[None, None, :]).astype(jnp.float32)
    return jnp.einsum("pqt,vt->vpq", selector, kernel, precision=HIGHEST)


def blur_inner(values, matrix_y, matrix_z):
    values = jnp.einsum("vpq,vxqz->vxpz", matrix_y, values, precision=HIGHEST)
    return jnp.einsum("vxyq,vpq->vxyp", values, matrix_z, precision=HIGHEST)


def unblur_inner(values, matrix_y, matrix_z):
    values = jnp.einsum("vqp,vxqz->vxpz", matrix_y, values, precision=HIGHEST)
    return jnp.einsum("vxyq,vqp->vxyp", values, matrix_z, precision=HIGHEST)


def blur_along_x(values, kernel_x, flipped):
    length = values.shape[1]
    padded = jnp.pad(values, ((0, 0), (HALF, HALF), (0, 0), (0, 0)))
    weights = kernel_x[:, ::-1] if flipped else kernel_x
    result = jnp.zeros(values.shape, jnp.float32)
    for offset in range(TAPS):
        result = result + weights[:, offset][:, None, None, None] * padded[:, offset:offset + length]
    return result


def view_product(correction):
    factor = correction[0]
    for member in range(1, correction.shape[0]):
        factor = factor * correction[member]
    return factor


def reference(measured, psf, stem_params, conv_weight, head_params):
    kernels = psf / jnp.sum(psf, axis=-1, keepdims=True)
    matrix_y = band_matrix(kernels[:, 1], CY, CY, HALF)
    matrix_z = band_matrix(kernels[:, 2], NZ, NZ, HALF)
    observed = measured.astype(jnp.float32)
    estimate = jnp.mean(observed, axis=0)
    for iteration in range(ITERS):
        spread_out = jnp.broadcast_to(estimate[None], observed.shape)
        blurred = blur_inner(blur_along_x(spread_out, kernels[:, 0], False), matrix_y, matrix_z)
        partial_value = unblur_inner(observed / blurred, matrix_y, matrix_z)
        correction = blur_along_x(partial_value, kernels[:, 0], True)
        estimate = estimate * view_product(correction)
    cell_count = NX * CY * NZ
    normal = estimate * (cell_count / jnp.sum(estimate))
    padded = jnp.pad(normal, ((1, 1), (0, 0), (0, 0)))
    conv_kernel = conv_weight.astype(jnp.float32).reshape(3, 3, 3, CH, CH).transpose(4, 3, 0, 1, 2)

    def block_logits(first_plane):
        window = lax.dynamic_slice_in_dim(padded, first_plane, 66, 0)
        planes = first_plane + jnp.arange(66, dtype=jnp.int32) - 1
        inside = ((planes >= 0) & (planes < NX)).astype(jnp.float32)
        features = jax.nn.relu(stem_params[0][:, None, None, None] * window[None] + stem_params[1][:, None, None, None])
        features = (features * inside[None, :, None, None]).astype(jnp.bfloat16)
        features = lax.optimization_barrier(features).astype(jnp.float32)
        response = lax.conv_general_dilated(features[None], conv_kernel, (1, 1, 1), ((0, 0), (1, 1), (1, 1)), dimension_numbers=("NCDHW", "OIDHW", "NCDHW"), precision=HIGHEST, preferred_element_type=jnp.float32)[0]
        hidden = jax.nn.relu(response + head_params[0][:, None, None, None])
        return jnp.einsum("c,cxyz->xyz", head_params[1], hidden, precision=HIGHEST)

    starts = jnp.arange(NX // 64, dtype=jnp.int32) * 64
    logits = lax.map(block_logits, starts).reshape(NX, CY, NZ)
    return estimate, logits
```

```python
import functools
import jax
import jax.numpy as jnp
from jax import lax
from jax.experimental import pallas as pl
from jax.experimental.pallas import tpu as pltpu
from jax.sharding import PartitionSpec as P

ITERS = 2


HIGHEST = lax.Precision.HIGHEST


def with_halo(cells, sides, width):
    for axis, dim in sides:
        count = lax.axis_size(axis)
        ends = count - 1
        head = lax.slice_in_dim(cells, 0, width, axis=dim)
        tail = lax.slice_in_dim(cells, cells.shape[dim] - width, cells.shape[dim], axis=dim)
        cells = jnp.concatenate(
            [
                lax.ppermute(tail, axis, [(i, (i + 1) % count) for i in range(ends)]),
                cells,
                lax.ppermute(head, axis, [((i + 1) % count, i) for i in range(ends)]),
            ],
            axis=dim,
        )
    return cells


def band_matrix(kernel, row_count, col_count, offset):
    spacing = (
        jnp.arange(col_count, dtype=jnp.int32)[None, :]
        - jnp.arange(row_count, dtype=jnp.int32)[:, None]
        + offset
    )
    selector = (
        spacing[:, :, None] == jnp.arange(kernel.shape[-1], dtype=jnp.int32)[None, None, :]
    ).astype(jnp.float32)
    return jnp.einsum("pqt,vt->vpq", selector, kernel, precision=HIGHEST)


def blur_inner(values, matrix_y, matrix_z):
    values = jnp.einsum("vpq,vxqz->vxpz", matrix_y, values, precision=HIGHEST)
    return jnp.einsum("vxyq,vpq->vxyp", values, matrix_z, precision=HIGHEST)


def unblur_inner(values, matrix_y, matrix_z):
    values = jnp.einsum("vqp,vxqz->vxpz", matrix_y, values, precision=HIGHEST)
    return jnp.einsum("vxyq,vqp->vxyp", values, matrix_z, precision=HIGHEST)


def view_product(correction):
    factor = correction[0]
    for member in range(1, correction.shape[0]):
        factor = factor * correction[member]
    return factor


YB = 8


def conv_matrix(conv_weight, yb=YB):
    ch = conv_weight.shape[1]
    w = conv_weight.reshape(3, 3, 3, ch, ch)
    rows = []
    for yo in range(yb):
        rows.append(jnp.pad(w, ((0, 0), (yo, yb - 1 - yo), (0, 0), (0, 0), (0, 0))))
    m = jnp.stack(rows, 0)
    m = m.transpose(1, 5, 0, 2, 3, 4)
    return m.reshape(3 * ch * yb, (yb + 2) * 3 * ch)


def conv_kernel(yb, count, tot_ref, flag_ref, head_ref, est_ref, stem_ref, w_ref, out_ref, n_ref, f_ref, c_ref):
    planes = est_ref.shape[0] // 32
    ch = stem_ref.shape[1]
    total = tot_ref[0]
    for k in range(1, tot_ref.shape[0]):
        total = total + tot_ref[k]
    scale = count / jnp.full((8, 128), total, jnp.float32)
    lane = lax.broadcasted_iota(jnp.int32, (ch, 128), 1)
    w0, b0 = stem_ref[0], stem_ref[1]
    keep = [lane > 0, None, lane < 127]
    wz = [w0 if k is None else jnp.where(k, w0, 0.0) for k in keep]
    bz = [b0 if k is None else jnp.where(k, b0, 0.0) for k in keep]

    def norm(e, _):
        at = pl.multiple_of(e * 32, 32)
        v = est_ref[pl.ds(at, 32), :]
        v = (v.reshape(4, 8, 128) * scale[None]).reshape(32, 128)
        n_ref[1, pl.ds(at, 32), :] = v
        n_ref[0, pl.ds(at, 32), :] = pltpu.roll(v, 1, 1)
        n_ref[2, pl.ds(at, 32), :] = pltpu.roll(v, 127, 1)
        return 0

    lax.fori_loop(0, planes, norm, 0)
    f_ref[0:48, :] = jnp.zeros((48, 256), jnp.bfloat16)
    f_ref[33 * 48:34 * 48, :] = jnp.zeros((48, 256), jnp.bfloat16)
    m = ch * yb

    def pair(j, _):
        for s in range(2):
            e = 2 * j + s
            flag = jnp.where(e == 0, flag_ref[0], jnp.where(e == planes - 1, flag_ref[1], 1.0))
            at = pl.multiple_of(e * 32, 32)
            for dz in range(3):
                w, b = wz[dz] * flag, bz[dz] * flag
                for y in range(32):
                    row = jnp.broadcast_to(n_ref[dz, pl.ds(at + y, 1), :], (ch, 128))
                    f = jnp.maximum(w * row + b, 0.0).astype(jnp.bfloat16)
                    f_ref[(y + 1) * 48 + dz * 16:(y + 1) * 48 + dz * 16 + 16, s * 128:(s + 1) * 128] = f
        for k in range(32 // yb):
            p = jnp.dot(w_ref[...], f_ref[k * yb * 48:k * yb * 48 + (yb + 2) * 48, :], preferred_element_type=jnp.float32)
            pm, p0, pp = p[:m], p[m:2 * m], p[2 * m:]
            old = c_ref[k]
            done0 = old[:, :128] + pp[:, :128]
            done1 = old[:, 128:] + p0[:, :128] + pp[:, 128:]
            c_ref[k, :, :128] = pm[:, :128] + p0[:, 128:]
            c_ref[k, :, 128:] = pm[:, 128:]

            @pl.when(j > 0)
            def _():
                for s, d in enumerate((done0, done1)):
                    acc = None
                    for c in range(ch):
                        h = jnp.maximum(d[c * yb:(c + 1) * yb] + head_ref[0, c], 0.0) * head_ref[1, c]
                        acc = h if acc is None else acc + h
                    out_ref[pl.ds(pl.multiple_of((2 * j - 2 + s) * 32 + k * yb, 8), yb), :] = acc
        return 0

    c_ref[...] = jnp.zeros_like(c_ref)
    lax.fori_loop(0, planes // 2, pair, 0)


def conv_call(totals, flags, head, est, stem, w, count, yb=YB):
    planes = est.shape[0] // 32
    ch = head.shape[1]
    smem = pl.BlockSpec(memory_space=pltpu.SMEM)
    vmem = pl.BlockSpec(memory_space=pltpu.VMEM)
    return pl.pallas_call(
        functools.partial(conv_kernel, yb, count),
        out_shape=jax.ShapeDtypeStruct(((planes - 2) * 32, 128), jnp.float32),
        in_specs=[smem, smem, smem, vmem, vmem, vmem],
        out_specs=vmem,
        scratch_shapes=[
            pltpu.VMEM((3, planes * 32, 128), jnp.float32),
            pltpu.VMEM((34 * 48, 256), jnp.bfloat16),
            pltpu.VMEM((32 // yb, ch * yb, 256), jnp.float32),
        ],
        compiler_params=pltpu.CompilerParams(vmem_limit_bytes=48 * 2**20),
        cost_estimate=pl.CostEstimate(flops=4 * 10**9, bytes_accessed=2 * 10**6, transcendentals=0),
        name="conv_head",
    )(totals, flags, head, est, stem, w)


def local(measured, psf, stem_params, conv_weight, head_params):
    plane_count = measured.shape[1]
    row_count = measured.shape[2]
    lane_count = measured.shape[3]
    half_reach = (psf.shape[-1] - 1) // 2
    kernels = psf / jnp.sum(psf, axis=-1, keepdims=True)
    matrix_y = band_matrix(kernels[:, 1], row_count, row_count, half_reach)
    matrix_z = band_matrix(kernels[:, 2], lane_count, lane_count, half_reach)
    behind_x = band_matrix(kernels[:, 0][:, ::-1], plane_count, plane_count + 2 * half_reach, 0)
    observed = measured.astype(jnp.float32)
    estimate = jnp.mean(observed, axis=0)
    ahead_x = band_matrix(kernels[:, 0], plane_count, plane_count + 2 * half_reach, 0)
    for iteration in range(ITERS):
        extended = with_halo(estimate, (("brick", 0),), half_reach)
        blurred = jnp.einsum("vpq,qyz->vpyz", ahead_x, extended, precision=HIGHEST)
        blurred = blur_inner(blurred, matrix_y, matrix_z)
        partial_value = unblur_inner(observed / blurred, matrix_y, matrix_z)
        partial_value = with_halo(partial_value, (("brick", 1),), half_reach)
        correction = jnp.einsum("vpq,vqyz->vpyz", behind_x, partial_value, precision=HIGHEST)
        estimate = estimate * view_product(correction)
    cell_count = lax.axis_size("brick") * plane_count * row_count * lane_count
    mine = jnp.broadcast_to(jnp.sum(estimate), (lax.axis_size("brick"),))
    totals = lax.all_to_all(mine, "brick", 0, 0, tiled=True)
    padded = with_halo(estimate, (("brick", 0),), 1)
    place = lax.axis_index("brick")
    flags = jnp.stack([place > 0, place < lax.axis_size("brick") - 1]).astype(jnp.float32)
    stem = jnp.broadcast_to(stem_params[:, :, None], stem_params.shape + (lane_count,))
    logits = conv_call(
        totals,
        flags,
        head_params,
        padded.reshape(-1, lane_count),
        stem,
        conv_matrix(conv_weight),
        float(cell_count),
    ).reshape(plane_count, row_count, lane_count)
    return (estimate, logits)


def solution(mesh):
    placed = (P(None, ("span", "brick"), None, None), P(), P(), P(), P())
    return jax.shard_map(
        local,
        mesh=mesh,
        in_specs=placed,
        out_specs=(P(("span", "brick"), None, None), P(("span", "brick"), None, None)),
        check_vma=False,
    )
```

```python
import functools
import jax, jax.numpy as jnp
from jax import lax
from jax.experimental import pallas as pl
from jax.experimental.pallas import tpu as pltpu
from jax.sharding import PartitionSpec as P

F32, BF16 = jnp.float32, jnp.bfloat16
HALO = 16
SMEM = pl.BlockSpec(memory_space=pltpu.SMEM)
VMEM = pl.BlockSpec(memory_space=pltpu.VMEM)


def iotas(shape):
    return lax.broadcasted_iota(jnp.int32, shape, 0), lax.broadcasted_iota(jnp.int32, shape, 1)


def bands(k_ref, dim, index):
    views, taps = k_ref.shape[0], k_ref.shape[2]
    out = [jnp.zeros(index.shape, F32)] * views
    for t in range(taps):
        hit = index == t
        out = [jnp.where(hit, k_ref[v, dim, t], out[v]) for v in range(views)]
    return out


def prep_kernel(k_ref, meas_ref, kx_ref, bz_ref, bzt_ref, ly_ref, lyt_ref, bxt_ref, bxt2_ref, meast_ref, est_ref, nat_ref):
    views = k_ref.shape[0]
    reach = (k_ref.shape[2] - 1) // 2
    r, c = iotas((64, 96))
    for v, m in enumerate(bands(k_ref, 0, c - r - HALO + reach)):
        kx_ref[v * 64:(v + 1) * 64, :] = m.astype(BF16)
    for ref, rows, first in ((bxt_ref, 32, 0), (bxt2_ref, 48, -8)):
        r, c = iotas((rows, 512))
        for v, m in enumerate(bands(k_ref, 0, (r + first) - ((c & 63) - HALO) + reach)):
            ref[v * rows:(v + 1) * rows, :] = jnp.where(((c >> 6) & 3) == v, m, 0.0).astype(BF16)
    r, c = iotas((128, 128))
    zero = jnp.zeros((128, 128), BF16)
    for ref, sign in ((bz_ref, 1), (bzt_ref, -1)):
        for v, m in enumerate(bands(k_ref, 2, sign * (r - c) + reach)):
            p, a = v // 2, v % 2
            ref[p, a * 128:(a + 1) * 128, a * 128:(a + 1) * 128] = m.astype(BF16)
            ref[p, a * 128:(a + 1) * 128, (1 - a) * 128:(2 - a) * 128] = zero
    r, c = iotas((32, 32))
    er, ec = iotas((256, 32))
    spread = ((er >> 3) == ec).astype(F32).astype(BF16)
    tr, tc = iotas((32, 256))
    spread_t = ((tc >> 3) == tr).astype(F32).astype(BF16)
    fr, fc = iotas((256, 256))
    same = (fr & 7) == (fc & 7)
    for ref, sign in ((ly_ref, 1), (lyt_ref, -1)):
        for v, m in enumerate(bands(k_ref, 1, sign * (c - r) + reach)):
            wide = jnp.dot(spread, m.astype(BF16), preferred_element_type=F32).astype(BF16)
            full = jnp.dot(wide, spread_t, preferred_element_type=F32)
            ref[v] = jnp.where(same, full, 0.0).astype(BF16)
    for v in range(views):
        nat_ref[v] = meas_ref[v].astype(F32)

    def turn(y, _):
        acc = None
        for v in range(views):
            m = nat_ref[v, pl.ds(y, 32, stride=32), :]
            acc = m if acc is None else acc + m
            meast_ref[v, y] = m.astype(BF16)
        est_ref[y] = acc * (1.0 / views)
        return 0

    lax.fori_loop(0, 32, turn, 0)


def prep_call(kernels, measured):
    views = measured.shape[0]
    out = [
        ((views * 64, 96), BF16),
        ((2, 256, 256), BF16),
        ((2, 256, 256), BF16),
        ((views, 256, 256), BF16),
        ((views, 256, 256), BF16),
        ((views * 32, 512), BF16),
        ((views * 48, 512), BF16),
        ((views, 32, 32, 128), BF16),
        ((32, 32, 128), F32),
    ]
    return pl.pallas_call(
        prep_kernel,
        out_shape=[jax.ShapeDtypeStruct(s, d) for s, d in out],
        in_specs=[SMEM, VMEM],
        out_specs=[VMEM] * len(out),
        scratch_shapes=[pltpu.VMEM((views, 1024, 128), F32)],
        compiler_params=pltpu.CompilerParams(vmem_limit_bytes=40 * 2**20),
        cost_estimate=pl.CostEstimate(flops=10**9, bytes_accessed=20 * 10**6, transcendentals=0),
        name="bands_and_turn",
    )(kernels, measured.reshape(views, 1024, 128))


def correct(eb_ref, meas, kx_ref, bz_ref, bzt_ref, ly_ref, lyt_ref, bxt_ref, rows, a_ref, b_ref, d_ref, finish):
    def ahead_x(i, _):
        y = i * 2
        both = jnp.concatenate([eb_ref[y], eb_ref[y + 1]], axis=1)
        p = jnp.dot(kx_ref[...], both, preferred_element_type=F32).astype(BF16)
        for v in range(4):
            a_ref[v, y] = p[v * 64:(v + 1) * 64, :128]
            a_ref[v, y + 1] = p[v * 64:(v + 1) * 64, 128:]
        return 0

    lax.fori_loop(0, 16, ahead_x, 0, unroll=2)

    def along_z(i, _):
        y = i * 4
        for p in range(2):
            both = jnp.concatenate([a_ref[2 * p + a, pl.ds(y, 4)].reshape(256, 128) for a in range(2)], axis=1)
            q = jnp.dot(both, bz_ref[p], preferred_element_type=F32)
            for a in range(2):
                b_ref[2 * p + a, pl.ds(y, 4)] = q[:, a * 128:(a + 1) * 128].reshape(4, 64, 128)
        return 0

    lax.fori_loop(0, 8, along_z, 0, unroll=2)

    for v in range(4):
        for k in range(4):
            x = k * 16
            halves = [b_ref[v, :, x + 8 * a:x + 8 * a + 8, :].reshape(256, 128).astype(BF16) for a in range(2)]
            q = jnp.dot(ly_ref[v], jnp.concatenate(halves, axis=1), preferred_element_type=F32)
            m = meas[v, :, x:x + 16, :].astype(F32)
            halves = []
            for a in range(2):
                top = m[:, 8 * a:8 * a + 8, :].reshape(256, 128)
                ratio = jnp.where(top > 0.0, top / q[:, a * 128:(a + 1) * 128], 0.0)
                halves.append(ratio.astype(BF16))
            q = jnp.dot(lyt_ref[v], jnp.concatenate(halves, axis=1), preferred_element_type=F32)
            halves = [q[:, a * 128:(a + 1) * 128].reshape(32, 8, 128) for a in range(2)]
            a_ref[v, :, x:x + 16, :] = jnp.concatenate(halves, axis=1).astype(BF16)

    def back_z(i, _):
        y = i * 4
        for p in range(2):
            both = jnp.concatenate([a_ref[2 * p + a, pl.ds(y, 4)].reshape(256, 128) for a in range(2)], axis=1)
            q = jnp.dot(both, bzt_ref[p], preferred_element_type=F32)
            for a in range(2):
                w = q[:, a * 128:(a + 1) * 128].reshape(4, 64, 128)
                hi = w.astype(BF16)
                at = (2 * p + a) * 64
                d_ref[pl.ds(y, 4), at:at + 64, :] = hi
                d_ref[pl.ds(y, 4), 256 + at:256 + at + 64, :] = (w - hi.astype(F32)).astype(BF16)
        return 0

    lax.fori_loop(0, 8, back_z, 0, unroll=2)

    def back_x(i, carry):
        y = i * 2
        both = jnp.concatenate([d_ref[y], d_ref[y + 1]], axis=1)
        p = jnp.dot(bxt_ref[...], both, preferred_element_type=F32)
        f = p[:rows]
        for v in range(1, 4):
            f = f * p[v * rows:(v + 1) * rows]
        carry = finish(y, f[:, :128], carry)
        return finish(y + 1, f[:, 128:], carry)

    return lax.fori_loop(0, 16, back_x, jnp.zeros((8, 128), F32), unroll=2)


def first_kernel(lo_ref, hi_ref, meast_ref, est_ref, kx, bz, bzt, ly, lyt, bxt, new_ref, newb_ref, measx_ref,
                 nat_ref, eb_ref, a_ref, b_ref, d_ref):
    for side, ref in enumerate((lo_ref, hi_ref)):
        for v in range(5):
            nat_ref[side, v] = ref[v].astype(F32)

    def turn(y, _):
        for side, near, far, at in ((0, 16, 0, 0), (1, 64, 80, 48)):
            acc = None
            for v in range(4):
                m = nat_ref[side, v, pl.ds(y, 16, stride=32), :]
                acc = m if acc is None else acc + m
                measx_ref[v, y, at:at + 16, :] = m.astype(BF16)
            eb_ref[y, near:near + 16, :] = (acc * 0.25).astype(BF16)
            eb_ref[y, far:far + 16, :] = nat_ref[side, 4, pl.ds(y, 16, stride=32), :].astype(BF16)
        for v in range(4):
            measx_ref[v, y, 16:48, :] = meast_ref[v, y]
        eb_ref[y, 32:64, :] = est_ref[y].astype(BF16)
        return 0

    lax.fori_loop(0, 32, turn, 0, unroll=2)

    def finish(y, f, carry):
        e = est_ref[y] * f
        new_ref[y] = e
        newb_ref[y] = e.astype(BF16)
        return carry

    correct(eb_ref, measx_ref, kx, bz, bzt, ly, lyt, bxt, 32, a_ref, b_ref, d_ref, finish)


def second_kernel(lo_ref, hi_ref, measx_ref, est_ref, kx, bz, bzt, ly, lyt, bxt, out_ref, ext_ref, sum_ref,
                  eb_ref, a_ref, b_ref, d_ref):
    def fill(y, _):
        eb_ref[y, 0:32, :] = lo_ref[y]
        eb_ref[y, 32:64, :] = est_ref[y].astype(BF16)
        eb_ref[y, 64:96, :] = hi_ref[y]
        return 0

    lax.fori_loop(0, 32, fill, 0, unroll=2)

    def finish(y, f, carry):
        mid = est_ref[y] * f[8:40]
        before = lo_ref[y, 16:32, :].astype(F32)[8:16] * f[0:8]
        after = hi_ref[y, 0:16, :].astype(F32)[0:8] * f[40:48]
        out_ref[pl.ds(y, 32, stride=32), :] = mid
        ext_ref[pl.ds(32 + y, 32, stride=32), :] = mid
        ext_ref[pl.ds(y, 1), :] = before[7:8]
        ext_ref[pl.ds(33 * 32 + y, 1), :] = after[0:1]
        return carry + ((mid[0:8] + mid[8:16]) + (mid[16:24] + mid[24:32]))

    total = correct(eb_ref, measx_ref, kx, bz, bzt, ly, lyt, bxt, 48, a_ref, b_ref, d_ref, finish)
    whole = jnp.sum(total)
    for k in range(sum_ref.shape[0]):
        sum_ref[k] = whole


SCRATCH = [
    pltpu.VMEM((32, 96, 128), BF16),
    pltpu.VMEM((4, 32, 64, 128), BF16),
    pltpu.VMEM((4, 32, 64, 128), F32),
    pltpu.VMEM((32, 512, 128), BF16),
]
COST = pl.CostEstimate(flops=6 * 10**9, bytes_accessed=8 * 10**6, transcendentals=0)


def first_call(lo, hi, meast, est, mats):
    return pl.pallas_call(
        first_kernel,
        out_shape=[
            jax.ShapeDtypeStruct((32, 32, 128), F32),
            jax.ShapeDtypeStruct((32, 32, 128), BF16),
            jax.ShapeDtypeStruct((4, 32, 64, 128), BF16),
        ],
        in_specs=[VMEM] * 10,
        out_specs=[VMEM] * 3,
        scratch_shapes=[pltpu.VMEM((2, 5, 512, 128), F32)] + SCRATCH,
        compiler_params=pltpu.CompilerParams(vmem_limit_bytes=48 * 2**20),
        cost_estimate=COST,
        name="first_iteration",
    )(lo.reshape(5, 512, 128), hi.reshape(5, 512, 128), meast, est, *mats)


def second_call(lo, hi, measx, est, mats, bricks):
    return pl.pallas_call(
        second_kernel,
        out_shape=[
            jax.ShapeDtypeStruct((1024, 128), F32),
            jax.ShapeDtypeStruct((34 * 32, 128), F32),
            jax.ShapeDtypeStruct((bricks,), F32),
        ],
        in_specs=[VMEM] * 10,
        out_specs=[VMEM, VMEM, SMEM],
        scratch_shapes=SCRATCH,
        compiler_params=pltpu.CompilerParams(vmem_limit_bytes=48 * 2**20),
        cost_estimate=COST,
        name="second_iteration",
    )(lo, hi, measx, est, *mats)

YB = 8


def conv_matrix(conv_weight, yb=YB):
    ch = conv_weight.shape[1]
    w = conv_weight.reshape(3, 3, 3, ch, ch)
    rows = []
    for yo in range(yb):
        rows.append(jnp.pad(w, ((0, 0), (yo, yb - 1 - yo), (0, 0), (0, 0), (0, 0))))
    m = jnp.stack(rows, 0)
    m = m.transpose(1, 5, 0, 2, 3, 4)
    return m.reshape(3 * ch * yb, (yb + 2) * 3 * ch)


def conv_kernel(yb, count, tot_ref, flag_ref, head_ref, est_ref, stem_ref, w_ref, out_ref, n_ref, f_ref, c_ref):
    planes = est_ref.shape[0] // 32
    ch = stem_ref.shape[1]
    total = tot_ref[0]
    for k in range(1, tot_ref.shape[0]):
        total = total + tot_ref[k]
    scale = count / jnp.full((8, 128), total, jnp.float32)
    lane = lax.broadcasted_iota(jnp.int32, (ch, 128), 1)
    w0, b0 = stem_ref[0], stem_ref[1]
    keep = [lane > 0, None, lane < 127]
    wz = [w0 if k is None else jnp.where(k, w0, 0.0) for k in keep]
    bz = [b0 if k is None else jnp.where(k, b0, 0.0) for k in keep]

    def norm(e, _):
        at = pl.multiple_of(e * 32, 32)
        v = est_ref[pl.ds(at, 32), :]
        v = (v.reshape(4, 8, 128) * scale[None]).reshape(32, 128)
        n_ref[1, pl.ds(at, 32), :] = v
        n_ref[0, pl.ds(at, 32), :] = pltpu.roll(v, 1, 1)
        n_ref[2, pl.ds(at, 32), :] = pltpu.roll(v, 127, 1)
        return 0

    lax.fori_loop(0, planes, norm, 0)
    f_ref[0:48, :] = jnp.zeros((48, 256), jnp.bfloat16)
    f_ref[33 * 48:34 * 48, :] = jnp.zeros((48, 256), jnp.bfloat16)
    m = ch * yb

    def pair(j, _):
        for s in range(2):
            e = 2 * j + s
            flag = jnp.where(e == 0, flag_ref[0], jnp.where(e == planes - 1, flag_ref[1], 1.0))
            at = pl.multiple_of(e * 32, 32)
            for dz in range(3):
                w, b = wz[dz] * flag, bz[dz] * flag
                for y in range(32):
                    row = jnp.broadcast_to(n_ref[dz, pl.ds(at + y, 1), :], (ch, 128))
                    f = jnp.maximum(w * row + b, 0.0).astype(jnp.bfloat16)
                    f_ref[(y + 1) * 48 + dz * 16:(y + 1) * 48 + dz * 16 + 16, s * 128:(s + 1) * 128] = f
        for k in range(32 // yb):
            p = jnp.dot(w_ref[...], f_ref[k * yb * 48:k * yb * 48 + (yb + 2) * 48, :], preferred_element_type=jnp.float32)
            pm, p0, pp = p[:m], p[m:2 * m], p[2 * m:]
            old = c_ref[k]
            done0 = old[:, :128] + pp[:, :128]
            done1 = old[:, 128:] + p0[:, :128] + pp[:, 128:]
            c_ref[k, :, :128] = pm[:, :128] + p0[:, 128:]
            c_ref[k, :, 128:] = pm[:, 128:]

            @pl.when(j > 0)
            def _():
                for s, d in enumerate((done0, done1)):
                    acc = None
                    for c in range(ch):
                        h = jnp.maximum(d[c * yb:(c + 1) * yb] + head_ref[0, c], 0.0) * head_ref[1, c]
                        acc = h if acc is None else acc + h
                    out_ref[pl.ds(pl.multiple_of((2 * j - 2 + s) * 32 + k * yb, 8), yb), :] = acc
        return 0

    c_ref[...] = jnp.zeros_like(c_ref)
    lax.fori_loop(0, planes // 2, pair, 0)


def conv_call(totals, flags, head, est, stem, w, count, yb=YB):
    planes = est.shape[0] // 32
    ch = head.shape[1]
    smem = pl.BlockSpec(memory_space=pltpu.SMEM)
    vmem = pl.BlockSpec(memory_space=pltpu.VMEM)
    return pl.pallas_call(
        functools.partial(conv_kernel, yb, count),
        out_shape=jax.ShapeDtypeStruct(((planes - 2) * 32, 128), jnp.float32),
        in_specs=[smem, smem, smem, vmem, vmem, vmem],
        out_specs=vmem,
        scratch_shapes=[
            pltpu.VMEM((3, planes * 32, 128), jnp.float32),
            pltpu.VMEM((34 * 48, 256), jnp.bfloat16),
            pltpu.VMEM((32 // yb, ch * yb, 256), jnp.float32),
        ],
        compiler_params=pltpu.CompilerParams(vmem_limit_bytes=48 * 2**20),
        cost_estimate=pl.CostEstimate(flops=4 * 10**9, bytes_accessed=2 * 10**6, transcendentals=0),
        name="conv_head",
    )(totals, flags, head, est, stem, w)


def shifted(cells, step):
    count = lax.axis_size("brick")
    pairs = [(i, i + step) for i in range(count) if 0 <= i + step < count]
    return lax.ppermute(cells, "brick", pairs)


def local(measured, psf, stem_params, conv_weight, head_params):
    views, plane_count, row_count, lane_count = measured.shape
    bricks = lax.axis_size("brick")
    early = jnp.mean(measured[:, :HALO].astype(F32), axis=0, keepdims=True).astype(BF16)
    late = jnp.mean(measured[:, HALO:].astype(F32), axis=0, keepdims=True).astype(BF16)
    lo = shifted(jnp.concatenate([measured[:, HALO:], early]), 1)
    hi = shifted(jnp.concatenate([measured[:, :HALO], late]), -1)
    kernels = psf / jnp.sum(psf, axis=-1, keepdims=True)
    *mats, bxt, bxt2, meast, est = prep_call(kernels, measured)
    est, estb, measx = first_call(lo, hi, meast, est, mats + [bxt])
    lo, hi = shifted(estb, 1), shifted(estb, -1)
    out, ext, mine = second_call(lo, hi, measx, est, mats + [bxt2], bricks)
    totals = lax.all_to_all(mine, "brick", 0, 0, tiled=True)
    place = lax.axis_index("brick")
    flags = jnp.stack([place > 0, place < bricks - 1]).astype(F32)
    stem = jnp.broadcast_to(stem_params[:, :, None], stem_params.shape + (lane_count,))
    cell_count = bricks * plane_count * row_count * lane_count
    logits = conv_call(totals, flags, head_params, ext, stem, conv_matrix(conv_weight), float(cell_count))
    shape = (plane_count, row_count, lane_count)
    return out.reshape(shape), logits.reshape(shape)


def solution(mesh):
    placed = (P(None, ("span", "brick"), None, None), P(), P(), P(), P())
    return jax.shard_map(
        local,
        mesh=mesh,
        in_specs=placed,
        out_specs=(P(("span", "brick"), None, None), P(("span", "brick"), None, None)),
        check_vma=False,
    )
```

```python
import functools
import jax, jax.numpy as jnp
from jax import lax
from jax.experimental import pallas as pl
from jax.experimental.pallas import tpu as pltpu
from jax.sharding import PartitionSpec as P

F32, BF16 = jnp.float32, jnp.bfloat16
HALO = 16
SMEM = pl.BlockSpec(memory_space=pltpu.SMEM)
VMEM = pl.BlockSpec(memory_space=pltpu.VMEM)


def iotas(shape):
    return lax.broadcasted_iota(jnp.int32, shape, 0), lax.broadcasted_iota(jnp.int32, shape, 1)


def bands(k_ref, dim, index):
    views, taps = k_ref.shape[0], k_ref.shape[2]
    out = [jnp.zeros(index.shape, F32)] * views
    for t in range(taps):
        hit = index == t
        out = [jnp.where(hit, k_ref[v, dim, t], out[v]) for v in range(views)]
    return out


def prep_kernel(k_ref, meas_ref, kx_ref, bz_ref, bzt_ref, ly_ref, lyt_ref, bxt_ref, bxt2_ref, meast_ref, est_ref, nat_ref):
    views = k_ref.shape[0]
    reach = (k_ref.shape[2] - 1) // 2
    r, c = iotas((64, 96))
    for v, m in enumerate(bands(k_ref, 0, c - r - HALO + reach)):
        kx_ref[v * 64:(v + 1) * 64, :] = m.astype(BF16)
    for ref, rows, first in ((bxt_ref, 32, 0), (bxt2_ref, 48, -8)):
        r, c = iotas((rows, 512))
        for v, m in enumerate(bands(k_ref, 0, (r + first) - ((c & 63) - HALO) + reach)):
            ref[v * rows:(v + 1) * rows, :] = jnp.where(((c >> 6) & 3) == v, m, 0.0).astype(BF16)
    r, c = iotas((128, 128))
    zero = jnp.zeros((128, 128), BF16)
    for ref, sign in ((bz_ref, 1), (bzt_ref, -1)):
        for v, m in enumerate(bands(k_ref, 2, sign * (r - c) + reach)):
            p, a = v // 2, v % 2
            ref[p, a * 128:(a + 1) * 128, a * 128:(a + 1) * 128] = m.astype(BF16)
            ref[p, a * 128:(a + 1) * 128, (1 - a) * 128:(2 - a) * 128] = zero
    r, c = iotas((32, 32))
    er, ec = iotas((256, 32))
    spread = ((er >> 3) == ec).astype(F32).astype(BF16)
    tr, tc = iotas((32, 256))
    spread_t = ((tc >> 3) == tr).astype(F32).astype(BF16)
    fr, fc = iotas((256, 256))
    same = (fr & 7) == (fc & 7)
    for ref, sign in ((ly_ref, 1), (lyt_ref, -1)):
        for v, m in enumerate(bands(k_ref, 1, sign * (c - r) + reach)):
            wide = jnp.dot(spread, m.astype(BF16), preferred_element_type=F32).astype(BF16)
            full = jnp.dot(wide, spread_t, preferred_element_type=F32)
            ref[v] = jnp.where(same, full, 0.0).astype(BF16)
    for v in range(views):
        nat_ref[v] = meas_ref[v].astype(F32)

    def turn(y, _):
        acc = None
        for v in range(views):
            m = nat_ref[v, pl.ds(y, 32, stride=32), :]
            acc = m if acc is None else acc + m
            meast_ref[v, y] = m.astype(BF16)
        est_ref[y] = acc * (1.0 / views)
        return 0

    lax.fori_loop(0, 32, turn, 0)


def prep_call(kernels, measured):
    views = measured.shape[0]
    out = [
        ((views * 64, 96), BF16),
        ((2, 256, 256), BF16),
        ((2, 256, 256), BF16),
        ((views, 256, 256), BF16),
        ((views, 256, 256), BF16),
        ((views * 32, 512), BF16),
        ((views * 48, 512), BF16),
        ((views, 32, 32, 128), BF16),
        ((32, 32, 128), F32),
    ]
    return pl.pallas_call(
        prep_kernel,
        out_shape=[jax.ShapeDtypeStruct(s, d) for s, d in out],
        in_specs=[SMEM, VMEM],
        out_specs=[VMEM] * len(out),
        scratch_shapes=[pltpu.VMEM((views, 1024, 128), F32)],
        compiler_params=pltpu.CompilerParams(vmem_limit_bytes=16 * 2**20),
        cost_estimate=pl.CostEstimate(flops=10**9, bytes_accessed=20 * 10**6, transcendentals=0),
        name="bands_and_turn",
    )(kernels, measured.reshape(views, 1024, 128))


XN, ZM, YN, XT = 8, 8, 8, 8


def correct(eb_ref, meas, kx_ref, bz_ref, bzt_ref, ly_ref, lyt_ref, bxt_ref, rows, a_ref, b_ref, c_ref, d_ref, finish):
    for k in range(32 // XN):
        at = k * XN * 128
        p = jnp.dot(kx_ref[...], eb_ref[:, at:at + XN * 128], preferred_element_type=F32)
        a_ref[:, at:at + XN * 128] = p.astype(BF16)

    for k in range(32 // ZM):
        for p in range(2):
            tall = []
            for y in range(k * ZM, k * ZM + ZM):
                tall.append(jnp.concatenate([a_ref[(2 * p + a) * 64:(2 * p + a) * 64 + 64, y * 128:y * 128 + 128] for a in range(2)], axis=1))
            q = jnp.dot(jnp.concatenate(tall, axis=0), bz_ref[p], preferred_element_type=F32)
            for a in range(2):
                b_ref[2 * p + a, k * ZM:k * ZM + ZM] = q[:, a * 128:(a + 1) * 128].reshape(ZM, 64, 128)

    for v in range(4):
        for k in range(8 // YN):
            x0 = k * YN * 8
            wide = [b_ref[v, :, x0 + 8 * a:x0 + 8 * a + 8, :].reshape(256, 128).astype(BF16) for a in range(YN)]
            q = jnp.dot(ly_ref[v], jnp.concatenate(wide, axis=1), preferred_element_type=F32)
            wide = []
            for h in range(YN // 2):
                m = meas[v, :, x0 + 16 * h:x0 + 16 * h + 16, :].astype(F32)
                for a in range(2):
                    top = m[:, 8 * a:8 * a + 8, :].reshape(256, 128)
                    at = (2 * h + a) * 128
                    ratio = jnp.where(top > 0.0, top / q[:, at:at + 128], 0.0)
                    wide.append(ratio.astype(BF16))
            q = jnp.dot(lyt_ref[v], jnp.concatenate(wide, axis=1), preferred_element_type=F32)
            for h in range(YN // 2):
                pair = [q[:, (2 * h + a) * 128:(2 * h + a + 1) * 128].reshape(32, 8, 128) for a in range(2)]
                c_ref[v, :, x0 + 16 * h:x0 + 16 * h + 16, :] = jnp.concatenate(pair, axis=1).astype(BF16)

    for k in range(32 // ZM):
        for p in range(2):
            tall = jnp.concatenate([c_ref[2 * p + a, k * ZM:k * ZM + ZM].reshape(ZM * 64, 128) for a in range(2)], axis=1)
            q = jnp.dot(tall, bzt_ref[p], preferred_element_type=F32)
            for a in range(2):
                at = (2 * p + a) * 64
                for y in range(ZM):
                    w = q[y * 64:y * 64 + 64, a * 128:(a + 1) * 128]
                    hi = w.astype(BF16)
                    col = (k * ZM + y) * 128
                    d_ref[at:at + 64, col:col + 128] = hi
                    d_ref[256 + at:256 + at + 64, col:col + 128] = (w - hi.astype(F32)).astype(BF16)

    carry = jnp.zeros((8, 128), F32)
    for k in range(32 // XT):
        p = jnp.dot(bxt_ref[...], d_ref[:, k * XT * 128:(k + 1) * XT * 128], preferred_element_type=F32)
        for y in range(XT):
            f = None
            for v in range(4):
                g = p[v * rows:(v + 1) * rows, y * 128:(y + 1) * 128]
                f = g if f is None else f * g
            carry = finish(k * XT + y, f, carry)
    return carry


def first_kernel(lo_ref, hi_ref, meast_ref, est_ref, kx, bz, bzt, ly, lyt, bxt, new_ref, newb_ref, measx_ref,
                 nat_ref, eb_ref, a_ref, b_ref, c_ref, d_ref):
    for side, ref in enumerate((lo_ref, hi_ref)):
        for v in range(5):
            nat_ref[side, v] = ref[v].astype(F32)

    def turn(y, _):
        col = pl.multiple_of(y * 128, 128)
        for side, near, far, at in ((0, 16, 0, 0), (1, 64, 80, 48)):
            acc = None
            for v in range(4):
                m = nat_ref[side, v, pl.ds(y, 16, stride=32), :]
                acc = m if acc is None else acc + m
                measx_ref[v, y, at:at + 16, :] = m.astype(BF16)
            eb_ref[near:near + 16, pl.ds(col, 128)] = (acc * 0.25).astype(BF16)
            eb_ref[far:far + 16, pl.ds(col, 128)] = nat_ref[side, 4, pl.ds(y, 16, stride=32), :].astype(BF16)
        for v in range(4):
            measx_ref[v, y, 16:48, :] = meast_ref[v, y]
        eb_ref[32:64, pl.ds(col, 128)] = est_ref[y].astype(BF16)
        return 0

    lax.fori_loop(0, 32, turn, 0, unroll=2)

    def finish(y, f, carry):
        e = est_ref[y] * f
        new_ref[y] = e
        newb_ref[y] = e.astype(BF16)
        return carry

    correct(eb_ref, measx_ref, kx, bz, bzt, ly, lyt, bxt, 32, a_ref, b_ref, c_ref, d_ref, finish)


def second_kernel(lo_ref, hi_ref, measx_ref, est_ref, kx, bz, bzt, ly, lyt, bxt, out_ref, ext_ref, sum_ref,
                  eb_ref, a_ref, b_ref, c_ref, d_ref):
    def fill(y, _):
        col = pl.multiple_of(y * 128, 128)
        eb_ref[0:32, pl.ds(col, 128)] = lo_ref[y]
        eb_ref[32:64, pl.ds(col, 128)] = est_ref[y].astype(BF16)
        eb_ref[64:96, pl.ds(col, 128)] = hi_ref[y]
        return 0

    lax.fori_loop(0, 32, fill, 0, unroll=2)

    def finish(y, f, carry):
        mid = est_ref[y] * f[8:40]
        before = lo_ref[y, 16:32, :].astype(F32)[8:16] * f[0:8]
        after = hi_ref[y, 0:16, :].astype(F32)[0:8] * f[40:48]
        out_ref[pl.ds(y, 32, stride=32), :] = mid
        ext_ref[pl.ds(32 + y, 32, stride=32), :] = mid
        ext_ref[pl.ds(y, 1), :] = before[7:8]
        ext_ref[pl.ds(33 * 32 + y, 1), :] = after[0:1]
        return carry + ((mid[0:8] + mid[8:16]) + (mid[16:24] + mid[24:32]))

    total = correct(eb_ref, measx_ref, kx, bz, bzt, ly, lyt, bxt, 48, a_ref, b_ref, c_ref, d_ref, finish)
    whole = jnp.sum(total)
    for k in range(sum_ref.shape[0]):
        sum_ref[k] = whole


SCRATCH = [
    pltpu.VMEM((96, 4096), BF16),
    pltpu.VMEM((256, 4096), BF16),
    pltpu.VMEM((4, 32, 64, 128), F32),
    pltpu.VMEM((4, 32, 64, 128), BF16),
    pltpu.VMEM((512, 4096), BF16),
]
COST = pl.CostEstimate(flops=6 * 10**9, bytes_accessed=8 * 10**6, transcendentals=0)


def first_call(lo, hi, meast, est, mats):
    return pl.pallas_call(
        first_kernel,
        out_shape=[
            jax.ShapeDtypeStruct((32, 32, 128), F32),
            jax.ShapeDtypeStruct((32, 32, 128), BF16),
            jax.ShapeDtypeStruct((4, 32, 64, 128), BF16),
        ],
        in_specs=[VMEM] * 10,
        out_specs=[VMEM] * 3,
        scratch_shapes=[pltpu.VMEM((2, 5, 512, 128), F32)] + SCRATCH,
        compiler_params=pltpu.CompilerParams(vmem_limit_bytes=32 * 2**20),
        cost_estimate=COST,
        name="first_iteration",
    )(lo.reshape(5, 512, 128), hi.reshape(5, 512, 128), meast, est, *mats)


def second_call(lo, hi, measx, est, mats, bricks):
    return pl.pallas_call(
        second_kernel,
        out_shape=[
            jax.ShapeDtypeStruct((1024, 128), F32),
            jax.ShapeDtypeStruct((34 * 32, 128), F32),
            jax.ShapeDtypeStruct((bricks,), F32),
        ],
        in_specs=[VMEM] * 10,
        out_specs=[VMEM, VMEM, SMEM],
        scratch_shapes=SCRATCH,
        compiler_params=pltpu.CompilerParams(vmem_limit_bytes=32 * 2**20),
        cost_estimate=COST,
        name="second_iteration",
    )(lo, hi, measx, est, *mats)

YB = 3


def conv_matrix(conv_weight, yb=YB):
    ch = conv_weight.shape[1]
    w = conv_weight.T.reshape(ch, 3, 9 * ch)
    step = 3 * ch
    rows = [jnp.pad(w, ((0, 0), (0, 0), (yo * step, (yb - 1 - yo) * step))) for yo in range(yb)]
    m = jnp.stack(rows, 0)
    return m.transpose(2, 0, 1, 3).reshape(3 * yb * ch, (yb + 2) * step)


def fold_channels(parts):
    sub = lax.broadcasted_iota(jnp.int32, (8, 128), 0)
    for width in (4, 2, 1):
        keep = (sub & width) == 0
        half = len(parts) // 2
        merged = []
        for k in range(half):
            a, b = parts[k], parts[k + half]
            swap = jnp.where(keep, b, a)
            merged.append(jnp.where(keep, a, b) + pltpu.roll(swap, width, 0) if width == 4 else
                          jnp.where(keep, a + pltpu.roll(a, 8 - width, 0), b + pltpu.roll(b, width, 0)))
        parts = merged
    return parts[0]


def conv_kernel(count, tot_ref, flag_ref, est_ref, stem_ref, head_ref, w_ref, out_ref, n_ref, f_ref, p_ref):
    planes = est_ref.shape[0] // 32
    ch = stem_ref.shape[1]
    total = tot_ref[0]
    for k in range(1, tot_ref.shape[0]):
        total = total + tot_ref[k]
    scale = count / jnp.full((8, 128), total, jnp.float32)
    lane = lax.broadcasted_iota(jnp.int32, (ch, 128), 1)
    w0, b0 = stem_ref[0], stem_ref[1]
    keep = [lane > 0, None, lane < 127]
    wz = [w0 if k is None else jnp.where(k, w0, 0.0) for k in keep]
    bz = [b0 if k is None else jnp.where(k, b0, 0.0) for k in keep]

    blank = jnp.zeros((48, planes * 128), jnp.bfloat16)
    for y in (0, 33, 34):
        f_ref[y * 48:(y + 1) * 48, :] = blank

    def plane(e, _):
        at = pl.multiple_of(e * 32, 32)
        col = pl.multiple_of(e * 128, 128)
        v = est_ref[pl.ds(at, 32), :]
        v = (v.reshape(4, 8, 128) * scale[None]).reshape(32, 128)
        n_ref[0] = pltpu.roll(v, 1, 1)
        n_ref[1] = v
        n_ref[2] = pltpu.roll(v, 127, 1)
        flag = jnp.where(e == 0, flag_ref[0], jnp.where(e == planes - 1, flag_ref[1], 1.0))
        for dz in range(3):
            w, b = wz[dz] * flag, bz[dz] * flag
            for y in range(32):
                row = jnp.broadcast_to(n_ref[dz, y:y + 1, :], (ch, 128))
                f = jnp.maximum(w * row + b, 0.0).astype(jnp.bfloat16)
                f_ref[(y + 1) * 48 + dz * 16:(y + 1) * 48 + dz * 16 + 16, pl.ds(col, 128)] = f
        return 0

    lax.fori_loop(0, planes, plane, 0)
    bias = [head_ref[0, 0:8], head_ref[0, 8:16]]
    gain = [head_ref[1, 0:8], head_ref[1, 8:16]]
    m = YB * ch

    def block(k, _):
        at = pl.multiple_of(k * (YB * 48), 16)
        p_ref[...] = jnp.dot(w_ref[...], f_ref[pl.ds(at, (YB + 2) * 48), :], preferred_element_type=jnp.float32)
        for yo in range(YB):
            rows = []
            for g in range((planes - 2) // 8):
                parts = []
                for o in range(g * 8, g * 8 + 8):
                    s = None
                    for h in range(2):
                        top = yo * ch + h * 8
                        acc = (p_ref[top:top + 8, o * 128:o * 128 + 128]
                               + p_ref[m + top:m + top + 8, o * 128 + 128:o * 128 + 256]
                               + p_ref[2 * m + top:2 * m + top + 8, o * 128 + 256:o * 128 + 384])
                        acc = jnp.maximum(acc + bias[h], 0.0) * gain[h]
                        s = acc if s is None else s + acc
                    parts.append(s)
                rows.append(fold_channels(parts))

            def put():
                for g, r in enumerate(rows):
                    out_ref[pl.ds(g * 256 + k * YB + yo, 8, stride=32), :] = r

            if yo == YB - 1:
                pl.when(k * YB + yo < 32)(put)
            else:
                put()
        return 0

    lax.fori_loop(0, 11, block, 0)


def conv_call(totals, flags, head, est, stem, w, count):
    planes = est.shape[0] // 32
    ch = head.shape[1]
    smem = pl.BlockSpec(memory_space=pltpu.SMEM)
    vmem = pl.BlockSpec(memory_space=pltpu.VMEM)
    return pl.pallas_call(
        functools.partial(conv_kernel, count),
        out_shape=jax.ShapeDtypeStruct(((planes - 2) * 32, 128), jnp.float32),
        in_specs=[smem, smem, vmem, vmem, vmem, vmem],
        out_specs=vmem,
        scratch_shapes=[
            pltpu.VMEM((3, 32, 128), jnp.float32),
            pltpu.VMEM((35 * 48, planes * 128), jnp.bfloat16),
            pltpu.VMEM((3 * YB * ch, planes * 128), jnp.float32),
        ],
        compiler_params=pltpu.CompilerParams(vmem_limit_bytes=40 * 2**20),
        cost_estimate=pl.CostEstimate(flops=4 * 10**9, bytes_accessed=2 * 10**6, transcendentals=0),
        name="conv_head",
    )(totals, flags, est, stem, jnp.broadcast_to(head[:, :, None], (2, ch, 128)), w)


def shifted(cells, step):
    count = lax.axis_size("brick")
    pairs = [(i, i + step) for i in range(count) if 0 <= i + step < count]
    return lax.ppermute(cells, "brick", pairs)


def local(measured, psf, stem_params, conv_weight, head_params):
    views, plane_count, row_count, lane_count = measured.shape
    bricks = lax.axis_size("brick")
    early = jnp.mean(measured[:, :HALO].astype(F32), axis=0, keepdims=True).astype(BF16)
    late = jnp.mean(measured[:, HALO:].astype(F32), axis=0, keepdims=True).astype(BF16)
    lo = shifted(jnp.concatenate([measured[:, HALO:], early]), 1)
    hi = shifted(jnp.concatenate([measured[:, :HALO], late]), -1)
    kernels = psf / jnp.sum(psf, axis=-1, keepdims=True)
    *mats, bxt, bxt2, meast, est = prep_call(kernels, measured)
    est, estb, measx = first_call(lo, hi, meast, est, mats + [bxt])
    lo, hi = shifted(estb, 1), shifted(estb, -1)
    out, ext, mine = second_call(lo, hi, measx, est, mats + [bxt2], bricks)
    totals = lax.all_to_all(mine, "brick", 0, 0, tiled=True)
    place = lax.axis_index("brick")
    flags = jnp.stack([place > 0, place < bricks - 1]).astype(F32)
    stem = jnp.broadcast_to(stem_params[:, :, None], stem_params.shape + (lane_count,))
    cell_count = bricks * plane_count * row_count * lane_count
    logits = conv_call(totals, flags, head_params, ext, stem, conv_matrix(conv_weight), float(cell_count))
    shape = (plane_count, row_count, lane_count)
    return out.reshape(shape), logits.reshape(shape)


def solution(mesh):
    placed = (P(None, ("span", "brick"), None, None), P(), P(), P(), P())
    return jax.shard_map(
        local,
        mesh=mesh,
        in_specs=placed,
        out_specs=(P(("span", "brick"), None, None), P(("span", "brick"), None, None)),
        check_vma=False,
    )
```

```python
import functools
import jax, jax.numpy as jnp
from jax import lax
from jax.experimental import pallas as pl
from jax.experimental.pallas import tpu as pltpu
from jax.sharding import PartitionSpec as P

F32, BF16 = jnp.float32, jnp.bfloat16
HALO = 16
SMEM = pl.BlockSpec(memory_space=pltpu.SMEM)
VMEM = pl.BlockSpec(memory_space=pltpu.VMEM)


def iotas(shape):
    return lax.broadcasted_iota(jnp.int32, shape, 0), lax.broadcasted_iota(jnp.int32, shape, 1)


def bands(k_ref, dim, index):
    views, taps = k_ref.shape[0], k_ref.shape[2]
    out = [jnp.zeros(index.shape, F32)] * views
    for t in range(taps):
        hit = index == t
        out = [jnp.where(hit, k_ref[v, dim, t], out[v]) for v in range(views)]
    return out


def prep_kernel(k_ref, meas_ref, kx_ref, bz_ref, bzt_ref, ly_ref, lyt_ref, bxt_ref, bxt2_ref, meast_ref, est_ref, nat_ref):
    views = k_ref.shape[0]
    reach = (k_ref.shape[2] - 1) // 2
    r, c = iotas((64, 96))
    for v, m in enumerate(bands(k_ref, 0, c - r - HALO + reach)):
        kx_ref[v * 64:(v + 1) * 64, :] = m.astype(BF16)
    for ref, rows, first in ((bxt_ref, 32, 0), (bxt2_ref, 48, -8)):
        r, c = iotas((rows, 512))
        for v, m in enumerate(bands(k_ref, 0, (r + first) - ((c & 63) - HALO) + reach)):
            ref[v * rows:(v + 1) * rows, :] = jnp.where(((c >> 6) & 3) == v, m, 0.0).astype(BF16)
    r, c = iotas((128, 128))
    zero = jnp.zeros((128, 128), BF16)
    for ref, sign in ((bz_ref, 1), (bzt_ref, -1)):
        for v, m in enumerate(bands(k_ref, 2, sign * (r - c) + reach)):
            p, a = v // 2, v % 2
            ref[p, a * 128:(a + 1) * 128, a * 128:(a + 1) * 128] = m.astype(BF16)
            ref[p, a * 128:(a + 1) * 128, (1 - a) * 128:(2 - a) * 128] = zero
    r, c = iotas((32, 32))
    er, ec = iotas((256, 32))
    spread = ((er >> 3) == ec).astype(F32).astype(BF16)
    tr, tc = iotas((32, 256))
    spread_t = ((tc >> 3) == tr).astype(F32).astype(BF16)
    fr, fc = iotas((256, 256))
    same = (fr & 7) == (fc & 7)
    for ref, sign in ((ly_ref, 1), (lyt_ref, -1)):
        for v, m in enumerate(bands(k_ref, 1, sign * (c - r) + reach)):
            wide = jnp.dot(spread, m.astype(BF16), preferred_element_type=F32).astype(BF16)
            full = jnp.dot(wide, spread_t, preferred_element_type=F32)
            ref[v] = jnp.where(same, full, 0.0).astype(BF16)
    for v in range(views):
        nat_ref[v] = meas_ref[v].astype(F32)

    def turn(y, _):
        acc = None
        for v in range(views):
            m = nat_ref[v, pl.ds(y, 32, stride=32), :]
            acc = m if acc is None else acc + m
            meast_ref[v, y] = m.astype(BF16)
        est_ref[y] = acc * (1.0 / views)
        return 0

    lax.fori_loop(0, 32, turn, 0)


def prep_call(kernels, measured):
    views = measured.shape[0]
    out = [
        ((views * 64, 96), BF16),
        ((2, 256, 256), BF16),
        ((2, 256, 256), BF16),
        ((views, 256, 256), BF16),
        ((views, 256, 256), BF16),
        ((views * 32, 512), BF16),
        ((views * 48, 512), BF16),
        ((views, 32, 32, 128), BF16),
        ((32, 32, 128), F32),
    ]
    return pl.pallas_call(
        prep_kernel,
        out_shape=[jax.ShapeDtypeStruct(s, d) for s, d in out],
        in_specs=[SMEM, VMEM],
        out_specs=[VMEM] * len(out),
        scratch_shapes=[pltpu.VMEM((views, 1024, 128), F32)],
        compiler_params=pltpu.CompilerParams(vmem_limit_bytes=16 * 2**20),
        cost_estimate=pl.CostEstimate(flops=10**9, bytes_accessed=20 * 10**6, transcendentals=0),
        name="bands_and_turn",
    )(kernels, measured.reshape(views, 1024, 128))


def message_kernel(meas_ref, up_ref, down_ref):
    views, rows = meas_ref.shape[0], meas_ref.shape[1] // 2
    for ref, near, far in ((up_ref, rows, 0), (down_ref, 0, rows)):
        acc = None
        for v in range(views):
            ref[v] = meas_ref[v, near:near + rows, :]
            m = meas_ref[v, far:far + rows, :].astype(F32)
            acc = m if acc is None else acc + m
        ref[views] = (acc * (1.0 / views)).astype(BF16)


def message_call(measured):
    views, rows, _ = measured.shape
    shape = jax.ShapeDtypeStruct((views + 1, rows // 2, 128), BF16)
    return pl.pallas_call(
        message_kernel,
        out_shape=[shape, shape],
        in_specs=[VMEM],
        out_specs=[VMEM, VMEM],
        compiler_params=pltpu.CompilerParams(vmem_limit_bytes=16 * 2**20),
        name="halo_messages",
    )(measured)


XN, ZM, YN, XT = 8, 8, 8, 8


def correct(eb_ref, meas, kx_ref, bz_ref, bzt_ref, ly_ref, lyt_ref, bxt_ref, rows, a_ref, b_ref, c_ref, d_ref, finish):
    for k in range(32 // XN):
        at = k * XN * 128
        p = jnp.dot(kx_ref[...], eb_ref[:, at:at + XN * 128], preferred_element_type=F32)
        a_ref[:, at:at + XN * 128] = p.astype(BF16)

    for k in range(32 // ZM):
        for p in range(2):
            tall = []
            for y in range(k * ZM, k * ZM + ZM):
                tall.append(jnp.concatenate([a_ref[(2 * p + a) * 64:(2 * p + a) * 64 + 64, y * 128:y * 128 + 128] for a in range(2)], axis=1))
            q = jnp.dot(jnp.concatenate(tall, axis=0), bz_ref[p], preferred_element_type=F32)
            for a in range(2):
                b_ref[2 * p + a, k * ZM:k * ZM + ZM] = q[:, a * 128:(a + 1) * 128].reshape(ZM, 64, 128)

    for v in range(4):
        for k in range(8 // YN):
            x0 = k * YN * 8
            wide = [b_ref[v, :, x0 + 8 * a:x0 + 8 * a + 8, :].reshape(256, 128).astype(BF16) for a in range(YN)]
            q = jnp.dot(ly_ref[v], jnp.concatenate(wide, axis=1), preferred_element_type=F32)
            wide = []
            for h in range(YN // 2):
                m = meas[v, :, x0 + 16 * h:x0 + 16 * h + 16, :].astype(F32)
                for a in range(2):
                    top = m[:, 8 * a:8 * a + 8, :].reshape(256, 128)
                    at = (2 * h + a) * 128
                    low = q[:, at:at + 128]
                    inverse = pl.reciprocal(low, approx=True)
                    ratio = top * (inverse * (2.0 - low * inverse))
                    if h in (0, YN // 2 - 1):
                        ratio = jnp.where(top > 0.0, ratio, 0.0)
                    wide.append(ratio.astype(BF16))
            q = jnp.dot(lyt_ref[v], jnp.concatenate(wide, axis=1), preferred_element_type=F32)
            for h in range(YN // 2):
                pair = [q[:, (2 * h + a) * 128:(2 * h + a + 1) * 128].reshape(32, 8, 128) for a in range(2)]
                c_ref[v, :, x0 + 16 * h:x0 + 16 * h + 16, :] = jnp.concatenate(pair, axis=1).astype(BF16)

    for k in range(32 // ZM):
        for p in range(2):
            tall = jnp.concatenate([c_ref[2 * p + a, k * ZM:k * ZM + ZM].reshape(ZM * 64, 128) for a in range(2)], axis=1)
            q = jnp.dot(tall, bzt_ref[p], preferred_element_type=F32)
            for a in range(2):
                at = (2 * p + a) * 64
                for y in range(ZM):
                    w = q[y * 64:y * 64 + 64, a * 128:(a + 1) * 128]
                    hi = w.astype(BF16)
                    col = (k * ZM + y) * 128
                    d_ref[at:at + 64, col:col + 128] = hi
                    d_ref[256 + at:256 + at + 64, col:col + 128] = (w - hi.astype(F32)).astype(BF16)

    carry = jnp.zeros((8, 128), F32)
    for k in range(32 // XT):
        p = jnp.dot(bxt_ref[...], d_ref[:, k * XT * 128:(k + 1) * XT * 128], preferred_element_type=F32)
        for y in range(XT):
            f = None
            for v in range(4):
                g = p[v * rows:(v + 1) * rows, y * 128:(y + 1) * 128]
                f = g if f is None else f * g
            carry = finish(k * XT + y, f, carry)
    return carry


def first_kernel(lo_ref, hi_ref, meast_ref, est_ref, kx, bz, bzt, ly, lyt, bxt, new_ref, newb_ref, measx_ref,
                 nat_ref, eb_ref, a_ref, b_ref, c_ref, d_ref):
    for side, ref in enumerate((lo_ref, hi_ref)):
        for v in range(5):
            nat_ref[side, v] = ref[v].astype(F32)

    def turn(y, _):
        col = pl.multiple_of(y * 128, 128)
        for side, near, far, at in ((0, 16, 0, 0), (1, 64, 80, 48)):
            acc = None
            for v in range(4):
                m = nat_ref[side, v, pl.ds(y, 16, stride=32), :]
                acc = m if acc is None else acc + m
                measx_ref[v, y, at:at + 16, :] = m.astype(BF16)
            eb_ref[near:near + 16, pl.ds(col, 128)] = (acc * 0.25).astype(BF16)
            eb_ref[far:far + 16, pl.ds(col, 128)] = nat_ref[side, 4, pl.ds(y, 16, stride=32), :].astype(BF16)
        for v in range(4):
            measx_ref[v, y, 16:48, :] = meast_ref[v, y]
        eb_ref[32:64, pl.ds(col, 128)] = est_ref[y].astype(BF16)
        return 0

    lax.fori_loop(0, 32, turn, 0, unroll=4)

    def finish(y, f, carry):
        e = est_ref[y] * f
        new_ref[y] = e
        newb_ref[y] = e.astype(BF16)
        return carry

    correct(eb_ref, measx_ref, kx, bz, bzt, ly, lyt, bxt, 32, a_ref, b_ref, c_ref, d_ref, finish)


def second_kernel(lo_ref, hi_ref, measx_ref, est_ref, kx, bz, bzt, ly, lyt, bxt, out_ref, ext_ref, sum_ref,
                  eb_ref, a_ref, b_ref, c_ref, d_ref):
    def fill(y, _):
        col = pl.multiple_of(y * 128, 128)
        eb_ref[0:32, pl.ds(col, 128)] = lo_ref[y]
        eb_ref[32:64, pl.ds(col, 128)] = est_ref[y].astype(BF16)
        eb_ref[64:96, pl.ds(col, 128)] = hi_ref[y]
        return 0

    lax.fori_loop(0, 32, fill, 0, unroll=4)

    def finish(y, f, carry):
        mid = est_ref[y] * f[8:40]
        before = lo_ref[y, 16:32, :].astype(F32)[8:16] * f[0:8]
        after = hi_ref[y, 0:16, :].astype(F32)[0:8] * f[40:48]
        out_ref[pl.ds(y, 32, stride=32), :] = mid
        ext_ref[pl.ds(32 + y, 32, stride=32), :] = mid
        ext_ref[pl.ds(y, 1), :] = before[7:8]
        ext_ref[pl.ds(33 * 32 + y, 1), :] = after[0:1]
        return carry + ((mid[0:8] + mid[8:16]) + (mid[16:24] + mid[24:32]))

    total = correct(eb_ref, measx_ref, kx, bz, bzt, ly, lyt, bxt, 48, a_ref, b_ref, c_ref, d_ref, finish)
    sum_ref[...] = jnp.broadcast_to(jnp.sum(total), sum_ref.shape)


SCRATCH = [
    pltpu.VMEM((96, 4096), BF16),
    pltpu.VMEM((256, 4096), BF16),
    pltpu.VMEM((4, 32, 64, 128), F32),
    pltpu.VMEM((4, 32, 64, 128), BF16),
    pltpu.VMEM((512, 4096), BF16),
]
COST = pl.CostEstimate(flops=6 * 10**9, bytes_accessed=8 * 10**6, transcendentals=0)


def first_call(lo, hi, meast, est, mats):
    return pl.pallas_call(
        first_kernel,
        out_shape=[
            jax.ShapeDtypeStruct((32, 32, 128), F32),
            jax.ShapeDtypeStruct((32, 32, 128), BF16),
            jax.ShapeDtypeStruct((4, 32, 64, 128), BF16),
        ],
        in_specs=[VMEM] * 10,
        out_specs=[VMEM] * 3,
        scratch_shapes=[pltpu.VMEM((2, 5, 512, 128), F32)] + SCRATCH,
        compiler_params=pltpu.CompilerParams(vmem_limit_bytes=32 * 2**20),
        cost_estimate=COST,
        name="first_iteration",
    )(lo.reshape(5, 512, 128), hi.reshape(5, 512, 128), meast, est, *mats)


def second_call(lo, hi, measx, est, mats, bricks):
    return pl.pallas_call(
        second_kernel,
        out_shape=[
            jax.ShapeDtypeStruct((1024, 128), F32),
            jax.ShapeDtypeStruct((34 * 32, 128), F32),
            jax.ShapeDtypeStruct((bricks, 1, 128), F32),
        ],
        in_specs=[VMEM] * 10,
        out_specs=[VMEM] * 3,
        scratch_shapes=SCRATCH,
        compiler_params=pltpu.CompilerParams(vmem_limit_bytes=32 * 2**20),
        cost_estimate=COST,
        name="second_iteration",
    )(lo, hi, measx, est, *mats)

YB = 3


def conv_matrix(conv_weight, yb=YB):
    ch = conv_weight.shape[1]
    w = conv_weight.T.reshape(ch, 3, 9 * ch)
    step = 3 * ch
    rows = [jnp.pad(w, ((0, 0), (0, 0), (yo * step, (yb - 1 - yo) * step))) for yo in range(yb)]
    m = jnp.stack(rows, 0)
    return m.transpose(2, 0, 1, 3).reshape(3 * yb * ch, (yb + 2) * step)


def fold_channels(parts):
    sub = lax.broadcasted_iota(jnp.int32, (8, 128), 0)
    for width in (4, 2, 1):
        keep = (sub & width) == 0
        half = len(parts) // 2
        merged = []
        for k in range(half):
            a, b = parts[k], parts[k + half]
            swap = jnp.where(keep, b, a)
            merged.append(jnp.where(keep, a, b) + pltpu.roll(swap, width, 0) if width == 4 else
                          jnp.where(keep, a + pltpu.roll(a, 8 - width, 0), b + pltpu.roll(b, width, 0)))
        parts = merged
    return parts[0]


def conv_kernel(count, tot_ref, flag_ref, est_ref, stem_ref, head_ref, w_ref, out_ref, n_ref, f_ref, *sums):
    planes = est_ref.shape[0] // 32
    ch = stem_ref.shape[1]
    scale = count / jnp.broadcast_to(jnp.sum(tot_ref[...], axis=0), (8, 128))
    lane = lax.broadcasted_iota(jnp.int32, (ch, 128), 1)
    w0, b0 = stem_ref[0], stem_ref[1]
    blank = jnp.zeros((48, planes * 128), jnp.bfloat16)
    for y in (0, 33, 34):
        f_ref[y * 48:(y + 1) * 48, :] = blank

    def plane(e, _):
        at = pl.multiple_of(e * 32, 32)
        col = pl.multiple_of(e * 128, 128)
        v = est_ref[pl.ds(at, 32), :]
        v = (v.reshape(4, 8, 128) * scale[None]).reshape(32, 128)
        n_ref[...] = v
        flag = jnp.where(e == 0, flag_ref[0], jnp.where(e == planes - 1, flag_ref[1], 1.0))
        w, b = w0 * flag, b0 * flag
        for y in range(32):
            row = n_ref[pl.ds(y, ch, stride=0), :]
            f = jnp.maximum(w * row + b, 0.0).astype(jnp.bfloat16)
            at = (y + 1) * 48
            f_ref[at:at + 16, pl.ds(col, 128)] = jnp.where(lane > 0, pltpu.roll(f, 1, 1), jnp.zeros_like(f))
            f_ref[at + 16:at + 32, pl.ds(col, 128)] = f
            f_ref[at + 32:at + 48, pl.ds(col, 128)] = jnp.where(lane < 127, pltpu.roll(f, 127, 1), jnp.zeros_like(f))
        return 0

    lax.fori_loop(0, planes, plane, 0, unroll=6)
    bias = [head_ref[0, 0:8], head_ref[0, 8:16]]
    gain = [head_ref[1, 0:8], head_ref[1, 8:16]]
    m = YB * ch

    for k in range(11):
        p_ref = sums[k % len(sums)]
        at = k * (YB * 48)
        p_ref[...] = jnp.dot(w_ref[...], f_ref[at:at + (YB + 2) * 48, :], preferred_element_type=jnp.float32)
        for yo in range(min(YB, 32 - k * YB)):
            for g in range((planes - 2) // 8):
                parts = []
                for o in range(g * 8, g * 8 + 8):
                    s = None
                    for h in range(2):
                        top = yo * ch + h * 8
                        acc = (p_ref[top:top + 8, o * 128:o * 128 + 128]
                               + p_ref[m + top:m + top + 8, o * 128 + 128:o * 128 + 256]
                               + p_ref[2 * m + top:2 * m + top + 8, o * 128 + 256:o * 128 + 384])
                        acc = jnp.maximum(acc + bias[h], 0.0) * gain[h]
                        s = acc if s is None else s + acc
                    parts.append(s)
                out_ref[pl.ds(g * 256 + k * YB + yo, 8, stride=32), :] = fold_channels(parts)


def conv_call(totals, flags, head, est, stem, w, count):
    planes = est.shape[0] // 32
    ch = head.shape[1]
    smem = pl.BlockSpec(memory_space=pltpu.SMEM)
    vmem = pl.BlockSpec(memory_space=pltpu.VMEM)
    return pl.pallas_call(
        functools.partial(conv_kernel, count),
        out_shape=jax.ShapeDtypeStruct(((planes - 2) * 32, 128), jnp.float32),
        in_specs=[vmem, smem, vmem, vmem, vmem, vmem],
        out_specs=vmem,
        scratch_shapes=[
            pltpu.VMEM((32, 128), jnp.float32),
            pltpu.VMEM((35 * 48, planes * 128), jnp.bfloat16),
        ] + [pltpu.VMEM((3 * YB * ch, planes * 128), jnp.float32)],
        compiler_params=pltpu.CompilerParams(vmem_limit_bytes=40 * 2**20),
        cost_estimate=pl.CostEstimate(flops=4 * 10**9, bytes_accessed=2 * 10**6, transcendentals=0),
        name="conv_head",
    )(totals, flags, est, stem, jnp.broadcast_to(head[:, :, None], (2, ch, 128)), w)


def shifted(cells, step):
    count = lax.axis_size("brick")
    pairs = [(i, i + step) for i in range(count) if 0 <= i + step < count]
    return lax.ppermute(cells, "brick", pairs)


def local(measured, psf, stem_params, conv_weight, head_params):
    views, plane_count, row_count, lane_count = measured.shape
    bricks = lax.axis_size("brick")
    up, down = message_call(measured.reshape(views, plane_count * row_count, lane_count))
    lo, hi = shifted(up, 1), shifted(down, -1)
    kernels = psf / jnp.sum(psf, axis=-1, keepdims=True)
    *mats, bxt, bxt2, meast, est = prep_call(kernels, measured)
    est, estb, measx = first_call(lo, hi, meast, est, mats + [bxt])
    lo, hi = shifted(estb, 1), shifted(estb, -1)
    out, ext, mine = second_call(lo, hi, measx, est, mats + [bxt2], bricks)
    totals = lax.all_to_all(mine, "brick", 0, 0, tiled=True)
    place = lax.axis_index("brick")
    flags = jnp.stack([place > 0, place < bricks - 1]).astype(F32)
    stem = jnp.broadcast_to(stem_params[:, :, None], stem_params.shape + (lane_count,))
    cell_count = bricks * plane_count * row_count * lane_count
    logits = conv_call(totals, flags, head_params, ext, stem, conv_matrix(conv_weight), float(cell_count))
    shape = (plane_count, row_count, lane_count)
    return out.reshape(shape), logits.reshape(shape)


def solution(mesh):
    placed = (P(None, ("span", "brick"), None, None), P(), P(), P(), P())
    return jax.shard_map(
        local,
        mesh=mesh,
        in_specs=placed,
        out_specs=(P(("span", "brick"), None, None), P(("span", "brick"), None, None)),
        check_vma=False,
    )
```

```python
import functools
import jax, jax.numpy as jnp
from jax import lax
from jax.experimental import pallas as pl
from jax.experimental.pallas import tpu as pltpu
from jax.sharding import PartitionSpec as P

F32, BF16 = jnp.float32, jnp.bfloat16
HALO = 16
SMEM = pl.BlockSpec(memory_space=pltpu.SMEM)
VMEM = pl.BlockSpec(memory_space=pltpu.VMEM)


def iotas(shape):
    return lax.broadcasted_iota(jnp.int32, shape, 0), lax.broadcasted_iota(jnp.int32, shape, 1)


def bands(k_ref, dim, index):
    views, taps = k_ref.shape[0], k_ref.shape[2]
    out = [jnp.zeros(index.shape, F32)] * views
    for t in range(taps):
        hit = index == t
        out = [jnp.where(hit, k_ref[v, dim, t], out[v]) for v in range(views)]
    return out


def prep_kernel(k_ref, meas_ref, w_ref, stem_ref, head_ref, flag_ref, kx_ref, bz_ref, bzt_ref, ly_ref, lyt_ref, bxt_ref, bxt2_ref, meast_ref, est_ref, nat_ref):
    views = k_ref.shape[0]
    reach = (k_ref.shape[2] - 1) // 2
    r, c = iotas((64, 96))
    for v, m in enumerate(bands(k_ref, 0, c - r - HALO + reach)):
        kx_ref[v * 64:(v + 1) * 64, :] = m.astype(BF16)
    for ref, rows, first in ((bxt_ref, 32, 0), (bxt2_ref, 48, -8)):
        r, c = iotas((rows, 512))
        for v, m in enumerate(bands(k_ref, 0, (r + first) - ((c & 63) - HALO) + reach)):
            ref[v * rows:(v + 1) * rows, :] = jnp.where(((c >> 6) & 3) == v, m, 0.0).astype(BF16)
    r, c = iotas((128, 128))
    zero = jnp.zeros((128, 128), BF16)
    for ref, sign in ((bz_ref, 1), (bzt_ref, -1)):
        for v, m in enumerate(bands(k_ref, 2, sign * (r - c) + reach)):
            p, a = v // 2, v % 2
            ref[p, a * 128:(a + 1) * 128, a * 128:(a + 1) * 128] = m.astype(BF16)
            ref[p, a * 128:(a + 1) * 128, (1 - a) * 128:(2 - a) * 128] = zero
    r, c = iotas((32, 32))
    er, ec = iotas((256, 32))
    spread = ((er >> 3) == ec).astype(F32).astype(BF16)
    tr, tc = iotas((32, 256))
    spread_t = ((tc >> 3) == tr).astype(F32).astype(BF16)
    fr, fc = iotas((256, 256))
    same = (fr & 7) == (fc & 7)
    for ref, sign in ((ly_ref, 1), (lyt_ref, -1)):
        for v, m in enumerate(bands(k_ref, 1, sign * (c - r) + reach)):
            wide = jnp.dot(spread, m.astype(BF16), preferred_element_type=F32).astype(BF16)
            full = jnp.dot(wide, spread_t, preferred_element_type=F32)
            ref[v] = jnp.where(same, full, 0.0).astype(BF16)
    for v in range(views):
        nat_ref[v] = meas_ref[v].astype(F32)

    def turn(y, _):
        acc = None
        for v in range(views):
            m = nat_ref[v, pl.ds(y, 32, stride=32), :]
            acc = m if acc is None else acc + m
            meast_ref[v, y] = m.astype(BF16)
        est_ref[y] = acc * (1.0 / views)
        return 0

    lax.fori_loop(0, 32, turn, 0)


def prep_call(kernels, measured, later):
    views = measured.shape[0]
    out = [
        ((views * 64, 96), BF16),
        ((2, 256, 256), BF16),
        ((2, 256, 256), BF16),
        ((views, 256, 256), BF16),
        ((views, 256, 256), BF16),
        ((views * 32, 512), BF16),
        ((views * 48, 512), BF16),
        ((views, 32, 32, 128), BF16),
        ((32, 32, 128), F32),
    ]
    return pl.pallas_call(
        prep_kernel,
        out_shape=[jax.ShapeDtypeStruct(s, d) for s, d in out],
        in_specs=[SMEM, VMEM] + [pl.BlockSpec(memory_space=pl.ANY)] * 4,
        out_specs=[VMEM] * len(out),
        scratch_shapes=[pltpu.VMEM((views, 1024, 128), F32)],
        compiler_params=pltpu.CompilerParams(vmem_limit_bytes=16 * 2**20),
        cost_estimate=pl.CostEstimate(flops=10**9, bytes_accessed=20 * 10**6, transcendentals=0),
        name="bands_and_turn",
    )(kernels, measured.reshape(views, 1024, 128), *later)


def message_kernel(meas_ref, up_ref, down_ref):
    views, rows = meas_ref.shape[0], meas_ref.shape[1] // 2
    for ref, near, far in ((up_ref, rows, 0), (down_ref, 0, rows)):
        acc = None
        for v in range(views):
            ref[v] = meas_ref[v, near:near + rows, :]
            m = meas_ref[v, far:far + rows, :].astype(F32)
            acc = m if acc is None else acc + m
        ref[views] = (acc * (1.0 / views)).astype(BF16)


def message_call(measured):
    views, rows, _ = measured.shape
    shape = jax.ShapeDtypeStruct((views + 1, rows // 2, 128), BF16)
    return pl.pallas_call(
        message_kernel,
        out_shape=[shape, shape],
        in_specs=[VMEM],
        out_specs=[VMEM, VMEM],
        compiler_params=pltpu.CompilerParams(vmem_limit_bytes=16 * 2**20),
        name="halo_messages",
    )(measured)


XN, ZM, YN, XT = 8, 8, 8, 8


def correct(eb_ref, meas, kx_ref, bz_ref, bzt_ref, ly_ref, lyt_ref, bxt_ref, rows, a_ref, b_ref, c_ref, d_ref, finish):
    for k in range(32 // XN):
        at = k * XN * 128
        p = jnp.dot(kx_ref[...], eb_ref[:, at:at + XN * 128], preferred_element_type=F32)
        a_ref[:, at:at + XN * 128] = p.astype(BF16)

    for k in range(32 // ZM):
        for p in range(2):
            tall = []
            for y in range(k * ZM, k * ZM + ZM):
                tall.append(jnp.concatenate([a_ref[(2 * p + a) * 64:(2 * p + a) * 64 + 64, y * 128:y * 128 + 128] for a in range(2)], axis=1))
            q = jnp.dot(jnp.concatenate(tall, axis=0), bz_ref[p], preferred_element_type=F32)
            for a in range(2):
                b_ref[2 * p + a, k * ZM:k * ZM + ZM] = q[:, a * 128:(a + 1) * 128].reshape(ZM, 64, 128)

    for v in range(4):
        for k in range(8 // YN):
            x0 = k * YN * 8
            wide = [b_ref[v, :, x0 + 8 * a:x0 + 8 * a + 8, :].reshape(256, 128).astype(BF16) for a in range(YN)]
            q = jnp.dot(ly_ref[v], jnp.concatenate(wide, axis=1), preferred_element_type=F32)
            wide = []
            for h in range(YN // 2):
                m = meas[v, :, x0 + 16 * h:x0 + 16 * h + 16, :].astype(F32)
                for a in range(2):
                    top = m[:, 8 * a:8 * a + 8, :].reshape(256, 128)
                    at = (2 * h + a) * 128
                    low = q[:, at:at + 128]
                    inverse = pl.reciprocal(low, approx=True)
                    ratio = top * (inverse * (2.0 - low * inverse))
                    if h in (0, YN // 2 - 1):
                        ratio = jnp.where(top > 0.0, ratio, 0.0)
                    wide.append(ratio.astype(BF16))
            q = jnp.dot(lyt_ref[v], jnp.concatenate(wide, axis=1), preferred_element_type=F32)
            for h in range(YN // 2):
                pair = [q[:, (2 * h + a) * 128:(2 * h + a + 1) * 128].reshape(32, 8, 128) for a in range(2)]
                c_ref[v, :, x0 + 16 * h:x0 + 16 * h + 16, :] = jnp.concatenate(pair, axis=1).astype(BF16)

    for k in range(32 // ZM):
        for p in range(2):
            tall = jnp.concatenate([c_ref[2 * p + a, k * ZM:k * ZM + ZM].reshape(ZM * 64, 128) for a in range(2)], axis=1)
            q = jnp.dot(tall, bzt_ref[p], preferred_element_type=F32)
            for a in range(2):
                at = (2 * p + a) * 64
                for y in range(ZM):
                    w = q[y * 64:y * 64 + 64, a * 128:(a + 1) * 128]
                    hi = w.astype(BF16)
                    col = (k * ZM + y) * 128
                    d_ref[at:at + 64, col:col + 128] = hi
                    d_ref[256 + at:256 + at + 64, col:col + 128] = (w - hi.astype(F32)).astype(BF16)

    carry = jnp.zeros((8, 128), F32)
    for k in range(32 // XT):
        p = jnp.dot(bxt_ref[...], d_ref[:, k * XT * 128:(k + 1) * XT * 128], preferred_element_type=F32)
        for y in range(XT):
            f = None
            for v in range(4):
                g = p[v * rows:(v + 1) * rows, y * 128:(y + 1) * 128]
                f = g if f is None else f * g
            carry = finish(k * XT + y, f, carry)
    return carry


def first_kernel(lo_ref, hi_ref, meast_ref, est_ref, kx, bz, bzt, ly, lyt, bxt, new_ref, newb_ref, measx_ref,
                 nat_ref, eb_ref, a_ref, b_ref, c_ref, d_ref):
    for side, ref in enumerate((lo_ref, hi_ref)):
        for v in range(5):
            nat_ref[side, v] = ref[v].astype(F32)

    def turn(y, _):
        col = pl.multiple_of(y * 128, 128)
        for side, near, far, at in ((0, 16, 0, 0), (1, 64, 80, 48)):
            acc = None
            for v in range(4):
                m = nat_ref[side, v, pl.ds(y, 16, stride=32), :]
                acc = m if acc is None else acc + m
                measx_ref[v, y, at:at + 16, :] = m.astype(BF16)
            eb_ref[near:near + 16, pl.ds(col, 128)] = (acc * 0.25).astype(BF16)
            eb_ref[far:far + 16, pl.ds(col, 128)] = nat_ref[side, 4, pl.ds(y, 16, stride=32), :].astype(BF16)
        for v in range(4):
            measx_ref[v, y, 16:48, :] = meast_ref[v, y]
        eb_ref[32:64, pl.ds(col, 128)] = est_ref[y].astype(BF16)
        return 0

    lax.fori_loop(0, 32, turn, 0, unroll=4)

    def finish(y, f, carry):
        e = est_ref[y] * f
        new_ref[y] = e
        newb_ref[y] = e.astype(BF16)
        return carry

    correct(eb_ref, measx_ref, kx, bz, bzt, ly, lyt, bxt, 32, a_ref, b_ref, c_ref, d_ref, finish)


def second_kernel(lo_ref, hi_ref, measx_ref, est_ref, kx, bz, bzt, ly, lyt, bxt, out_ref, ext_ref, sum_ref,
                  eb_ref, a_ref, b_ref, c_ref, d_ref):
    def fill(y, _):
        col = pl.multiple_of(y * 128, 128)
        eb_ref[0:32, pl.ds(col, 128)] = lo_ref[y]
        eb_ref[32:64, pl.ds(col, 128)] = est_ref[y].astype(BF16)
        eb_ref[64:96, pl.ds(col, 128)] = hi_ref[y]
        return 0

    lax.fori_loop(0, 32, fill, 0, unroll=4)

    def finish(y, f, carry):
        mid = est_ref[y] * f[8:40]
        before = lo_ref[y, 16:32, :].astype(F32)[8:16] * f[0:8]
        after = hi_ref[y, 0:16, :].astype(F32)[0:8] * f[40:48]
        out_ref[pl.ds(y, 32, stride=32), :] = mid
        ext_ref[pl.ds(32 + y, 32, stride=32), :] = mid
        ext_ref[pl.ds(y, 1), :] = before[7:8]
        ext_ref[pl.ds(33 * 32 + y, 1), :] = after[0:1]
        return carry + ((mid[0:8] + mid[8:16]) + (mid[16:24] + mid[24:32]))

    total = correct(eb_ref, measx_ref, kx, bz, bzt, ly, lyt, bxt, 48, a_ref, b_ref, c_ref, d_ref, finish)
    sum_ref[...] = jnp.broadcast_to(jnp.sum(total), sum_ref.shape)


SCRATCH = [
    pltpu.VMEM((96, 4096), BF16),
    pltpu.VMEM((256, 4096), BF16),
    pltpu.VMEM((4, 32, 64, 128), F32),
    pltpu.VMEM((4, 32, 64, 128), BF16),
    pltpu.VMEM((512, 4096), BF16),
]
COST = pl.CostEstimate(flops=6 * 10**9, bytes_accessed=8 * 10**6, transcendentals=0)


def first_call(lo, hi, meast, est, mats):
    return pl.pallas_call(
        first_kernel,
        out_shape=[
            jax.ShapeDtypeStruct((32, 32, 128), F32),
            jax.ShapeDtypeStruct((32, 32, 128), BF16),
            jax.ShapeDtypeStruct((4, 32, 64, 128), BF16),
        ],
        in_specs=[VMEM] * 10,
        out_specs=[VMEM] * 3,
        scratch_shapes=[pltpu.VMEM((2, 5, 512, 128), F32)] + SCRATCH,
        compiler_params=pltpu.CompilerParams(vmem_limit_bytes=32 * 2**20),
        cost_estimate=COST,
        name="first_iteration",
    )(lo.reshape(5, 512, 128), hi.reshape(5, 512, 128), meast, est, *mats)


def second_call(lo, hi, measx, est, mats, bricks):
    return pl.pallas_call(
        second_kernel,
        out_shape=[
            jax.ShapeDtypeStruct((1024, 128), F32),
            jax.ShapeDtypeStruct((34 * 32, 128), F32),
            jax.ShapeDtypeStruct((bricks, 1, 128), F32),
        ],
        in_specs=[VMEM] * 10,
        out_specs=[VMEM] * 3,
        scratch_shapes=SCRATCH,
        compiler_params=pltpu.CompilerParams(vmem_limit_bytes=32 * 2**20),
        cost_estimate=COST,
        name="second_iteration",
    )(lo, hi, measx, est, *mats)

YB = 3


def conv_matrix(conv_weight, yb=YB):
    ch = conv_weight.shape[1]
    w = conv_weight.T.reshape(ch, 3, 9 * ch)
    step = 3 * ch
    rows = [jnp.pad(w, ((0, 0), (0, 0), (yo * step, (yb - 1 - yo) * step))) for yo in range(yb)]
    m = jnp.stack(rows, 0)
    return m.transpose(2, 0, 1, 3).reshape(3 * yb * ch, (yb + 2) * step)


def fold_channels(parts):
    sub = lax.broadcasted_iota(jnp.int32, (8, 128), 0)
    for width in (4, 2, 1):
        keep = (sub & width) == 0
        half = len(parts) // 2
        merged = []
        for k in range(half):
            a, b = parts[k], parts[k + half]
            swap = jnp.where(keep, b, a)
            merged.append(jnp.where(keep, a, b) + pltpu.roll(swap, width, 0) if width == 4 else
                          jnp.where(keep, a + pltpu.roll(a, 8 - width, 0), b + pltpu.roll(b, width, 0)))
        parts = merged
    return parts[0]


def conv_kernel(count, tot_ref, flag_ref, est_ref, stem_ref, head_ref, w_ref, out_ref, n_ref, f_ref, *sums):
    planes = est_ref.shape[0] // 32
    ch = stem_ref.shape[1]
    scale = count / jnp.broadcast_to(jnp.sum(tot_ref[...], axis=0), (8, 128))
    lane = lax.broadcasted_iota(jnp.int32, (ch, 128), 1)
    w0, b0 = stem_ref[0], stem_ref[1]
    blank = jnp.zeros((48, planes * 128), jnp.bfloat16)
    for y in (0, 33, 34):
        f_ref[y * 48:(y + 1) * 48, :] = blank

    def plane(e, _):
        at = pl.multiple_of(e * 32, 32)
        col = pl.multiple_of(e * 128, 128)
        v = est_ref[pl.ds(at, 32), :]
        v = (v.reshape(4, 8, 128) * scale[None]).reshape(32, 128)
        n_ref[...] = v
        flag = jnp.where(e == 0, flag_ref[0], jnp.where(e == planes - 1, flag_ref[1], 1.0))
        w, b = w0 * flag, b0 * flag
        for y in range(32):
            row = n_ref[pl.ds(y, ch, stride=0), :]
            f = jnp.maximum(w * row + b, 0.0).astype(jnp.bfloat16)
            at = (y + 1) * 48
            f_ref[at:at + 16, pl.ds(col, 128)] = jnp.where(lane > 0, pltpu.roll(f, 1, 1), jnp.zeros_like(f))
            f_ref[at + 16:at + 32, pl.ds(col, 128)] = f
            f_ref[at + 32:at + 48, pl.ds(col, 128)] = jnp.where(lane < 127, pltpu.roll(f, 127, 1), jnp.zeros_like(f))
        return 0

    lax.fori_loop(0, planes, plane, 0, unroll=6)
    bias = [head_ref[0, 0:8], head_ref[0, 8:16]]
    gain = [head_ref[1, 0:8], head_ref[1, 8:16]]
    m = YB * ch

    for k in range(11):
        p_ref = sums[k % len(sums)]
        at = k * (YB * 48)
        p_ref[...] = jnp.dot(w_ref[...], f_ref[at:at + (YB + 2) * 48, :], preferred_element_type=jnp.float32)
        for yo in range(min(YB, 32 - k * YB)):
            for g in range((planes - 2) // 8):
                parts = []
                for o in range(g * 8, g * 8 + 8):
                    s = None
                    for h in range(2):
                        top = yo * ch + h * 8
                        acc = (p_ref[top:top + 8, o * 128:o * 128 + 128]
                               + p_ref[m + top:m + top + 8, o * 128 + 128:o * 128 + 256]
                               + p_ref[2 * m + top:2 * m + top + 8, o * 128 + 256:o * 128 + 384])
                        acc = jnp.maximum(acc + bias[h], 0.0) * gain[h]
                        s = acc if s is None else s + acc
                    parts.append(s)
                out_ref[pl.ds(g * 256 + k * YB + yo, 8, stride=32), :] = fold_channels(parts)


def conv_call(totals, est, later, count):
    w, stem, head, flags = later
    planes = est.shape[0] // 32
    ch = head.shape[1]
    smem = pl.BlockSpec(memory_space=pltpu.SMEM)
    vmem = pl.BlockSpec(memory_space=pltpu.VMEM)
    return pl.pallas_call(
        functools.partial(conv_kernel, count),
        out_shape=jax.ShapeDtypeStruct(((planes - 2) * 32, 128), jnp.float32),
        in_specs=[vmem, smem, vmem, vmem, vmem, vmem],
        out_specs=vmem,
        scratch_shapes=[
            pltpu.VMEM((32, 128), jnp.float32),
            pltpu.VMEM((35 * 48, planes * 128), jnp.bfloat16),
        ] + [pltpu.VMEM((3 * YB * ch, planes * 128), jnp.float32)],
        compiler_params=pltpu.CompilerParams(vmem_limit_bytes=40 * 2**20),
        cost_estimate=pl.CostEstimate(flops=4 * 10**9, bytes_accessed=2 * 10**6, transcendentals=0),
        name="conv_head",
    )(totals, flags, est, stem, head, w)


def shifted(cells, step):
    count = lax.axis_size("brick")
    pairs = [(i, i + step) for i in range(count) if 0 <= i + step < count]
    return lax.ppermute(cells, "brick", pairs)


def local(measured, psf, stem_params, conv_weight, head_params):
    views, plane_count, row_count, lane_count = measured.shape
    bricks = lax.axis_size("brick")
    up, down = message_call(measured.reshape(views, plane_count * row_count, lane_count))
    lo, hi = shifted(up, 1), shifted(down, -1)
    kernels = psf / jnp.sum(psf, axis=-1, keepdims=True)
    place = lax.axis_index("brick")
    flags = jnp.stack([place > 0, place < bricks - 1]).astype(F32)
    stem = jnp.broadcast_to(stem_params[:, :, None], stem_params.shape + (lane_count,))
    head = jnp.broadcast_to(head_params[:, :, None], head_params.shape + (lane_count,))
    later = (conv_matrix(conv_weight), stem, head, flags)
    *mats, bxt, bxt2, meast, est = prep_call(kernels, measured, later)
    est, estb, measx = first_call(lo, hi, meast, est, mats + [bxt])
    lo, hi = shifted(estb, 1), shifted(estb, -1)
    out, ext, mine = second_call(lo, hi, measx, est, mats + [bxt2], bricks)
    totals = lax.all_to_all(mine, "brick", 0, 0, tiled=True)
    cell_count = bricks * plane_count * row_count * lane_count
    logits = conv_call(totals, ext, later, float(cell_count))
    shape = (plane_count, row_count, lane_count)
    return out.reshape(shape), logits.reshape(shape)


def solution(mesh):
    placed = (P(None, ("span", "brick"), None, None), P(), P(), P(), P())
    return jax.shard_map(
        local,
        mesh=mesh,
        in_specs=placed,
        out_specs=(P(("span", "brick"), None, None), P(("span", "brick"), None, None)),
        check_vma=False,
    )
```

```python
import functools
import jax, jax.numpy as jnp
from jax import lax
from jax.experimental import pallas as pl
from jax.experimental.pallas import tpu as pltpu
from jax.sharding import PartitionSpec as P

F32, BF16 = jnp.float32, jnp.bfloat16
HALO = 16
SMEM = pl.BlockSpec(memory_space=pltpu.SMEM)
VMEM = pl.BlockSpec(memory_space=pltpu.VMEM)


def iotas(shape):
    return lax.broadcasted_iota(jnp.int32, shape, 0), lax.broadcasted_iota(jnp.int32, shape, 1)


def bands(k_ref, dim, index):
    views, taps = k_ref.shape[0], k_ref.shape[2]
    out = [jnp.zeros(index.shape, F32)] * views
    for t in range(taps):
        hit = index == t
        out = [jnp.where(hit, k_ref[v, dim, t], out[v]) for v in range(views)]
    return out


def prep_kernel(k_ref, meas_ref, w_ref, stem_ref, head_ref, flag_ref, kx_ref, bz_ref, bzt_ref, ly_ref, lyt_ref, bxt_ref, bxt2_ref, meast_ref, est_ref, nat_ref):
    views = k_ref.shape[0]
    reach = (k_ref.shape[2] - 1) // 2
    r, c = iotas((64, 96))
    for v, m in enumerate(bands(k_ref, 0, c - r - HALO + reach)):
        kx_ref[v * 64:(v + 1) * 64, :] = m.astype(BF16)
    for ref, rows, first in ((bxt_ref, 32, 0), (bxt2_ref, 48, -8)):
        r, c = iotas((rows, 512))
        for v, m in enumerate(bands(k_ref, 0, (r + first) - ((c & 63) - HALO) + reach)):
            ref[v * rows:(v + 1) * rows, :] = jnp.where(((c >> 6) & 3) == v, m, 0.0).astype(BF16)
    r, c = iotas((128, 128))
    zero = jnp.zeros((128, 128), BF16)
    for ref, sign in ((bz_ref, 1), (bzt_ref, -1)):
        for v, m in enumerate(bands(k_ref, 2, sign * (r - c) + reach)):
            p, a = v // 2, v % 2
            ref[p, a * 128:(a + 1) * 128, a * 128:(a + 1) * 128] = m.astype(BF16)
            ref[p, a * 128:(a + 1) * 128, (1 - a) * 128:(2 - a) * 128] = zero
    r, c = iotas((32, 32))
    er, ec = iotas((256, 32))
    spread = ((er >> 3) == ec).astype(F32).astype(BF16)
    tr, tc = iotas((32, 256))
    spread_t = ((tc >> 3) == tr).astype(F32).astype(BF16)
    fr, fc = iotas((256, 256))
    same = (fr & 7) == (fc & 7)
    for ref, sign in ((ly_ref, 1), (lyt_ref, -1)):
        for v, m in enumerate(bands(k_ref, 1, sign * (c - r) + reach)):
            wide = jnp.dot(spread, m.astype(BF16), preferred_element_type=F32).astype(BF16)
            full = jnp.dot(wide, spread_t, preferred_element_type=F32)
            ref[v] = jnp.where(same, full, 0.0).astype(BF16)
    for v in range(views):
        nat_ref[v] = meas_ref[v].astype(F32)

    def turn(y, _):
        acc = None
        for v in range(views):
            m = nat_ref[v, pl.ds(y, 32, stride=32), :]
            acc = m if acc is None else acc + m
            meast_ref[v, y] = m.astype(BF16)
        est_ref[y] = acc * (1.0 / views)
        return 0

    lax.fori_loop(0, 32, turn, 0)


def prep_call(kernels, measured, later):
    views = measured.shape[0]
    out = [
        ((views * 64, 96), BF16),
        ((2, 256, 256), BF16),
        ((2, 256, 256), BF16),
        ((views, 256, 256), BF16),
        ((views, 256, 256), BF16),
        ((views * 32, 512), BF16),
        ((views * 48, 512), BF16),
        ((views, 32, 32, 128), BF16),
        ((32, 32, 128), F32),
    ]
    return pl.pallas_call(
        prep_kernel,
        out_shape=[jax.ShapeDtypeStruct(s, d) for s, d in out],
        in_specs=[SMEM, VMEM] + [pl.BlockSpec(memory_space=pl.ANY)] * 4,
        out_specs=[VMEM] * len(out),
        scratch_shapes=[pltpu.VMEM((views, 1024, 128), F32)],
        compiler_params=pltpu.CompilerParams(vmem_limit_bytes=16 * 2**20),
        cost_estimate=pl.CostEstimate(flops=10**9, bytes_accessed=20 * 10**6, transcendentals=0),
        name="bands_and_turn",
    )(kernels, measured.reshape(views, 1024, 128), *later)


def message_kernel(meas_ref, up_ref, down_ref):
    views, rows = meas_ref.shape[0], meas_ref.shape[1] // 2
    for ref, near, far in ((up_ref, rows, 0), (down_ref, 0, rows)):
        acc = None
        for v in range(views):
            ref[v] = meas_ref[v, near:near + rows, :]
            m = meas_ref[v, far:far + rows, :].astype(F32)
            acc = m if acc is None else acc + m
        ref[views] = (acc * (1.0 / views)).astype(BF16)


def message_call(measured):
    views, rows, _ = measured.shape
    shape = jax.ShapeDtypeStruct((views + 1, rows // 2, 128), BF16)
    return pl.pallas_call(
        message_kernel,
        out_shape=[shape, shape],
        in_specs=[VMEM],
        out_specs=[VMEM, VMEM],
        compiler_params=pltpu.CompilerParams(vmem_limit_bytes=16 * 2**20),
        name="halo_messages",
    )(measured)


XN, ZM, YN, XT = 8, 8, 2, 8


def correct(eb_ref, meas, kx_ref, bz_ref, bzt_ref, ly_ref, lyt_ref, bxt_ref, rows, a_ref, b_ref, c_ref, d_ref, finish):
    for k in range(32 // XN):
        at = k * XN * 128
        p = jnp.dot(kx_ref[...], eb_ref[:, at:at + XN * 128], preferred_element_type=F32)
        a_ref[:, at:at + XN * 128] = p.astype(BF16)

    for k in range(32 // ZM):
        for p in range(2):
            tall = []
            for y in range(k * ZM, k * ZM + ZM):
                tall.append(jnp.concatenate([a_ref[(2 * p + a) * 64:(2 * p + a) * 64 + 64, y * 128:y * 128 + 128] for a in range(2)], axis=1))
            q = jnp.dot(jnp.concatenate(tall, axis=0), bz_ref[p], preferred_element_type=F32)
            for a in range(2):
                b_ref[2 * p + a, k * ZM:k * ZM + ZM] = q[:, a * 128:(a + 1) * 128].reshape(ZM, 64, 128)

    for v in range(4):
        for k in range(8 // YN):
            x0 = k * YN * 8
            wide = [b_ref[v, :, x0 + 8 * a:x0 + 8 * a + 8, :].reshape(256, 128).astype(BF16) for a in range(YN)]
            q = jnp.dot(ly_ref[v], jnp.concatenate(wide, axis=1), preferred_element_type=F32)
            wide = []
            for h in range(YN // 2):
                m = meas[v, :, x0 + 16 * h:x0 + 16 * h + 16, :].astype(F32)
                for a in range(2):
                    top = m[:, 8 * a:8 * a + 8, :].reshape(256, 128)
                    at = (2 * h + a) * 128
                    low = q[:, at:at + 128]
                    inverse = pl.reciprocal(low, approx=True)
                    ratio = top * (inverse * (2.0 - low * inverse))
                    if not HALO <= x0 + 16 * h < 64 - HALO:
                        ratio = jnp.where(top > 0.0, ratio, 0.0)
                    wide.append(ratio.astype(BF16))
            q = jnp.dot(lyt_ref[v], jnp.concatenate(wide, axis=1), preferred_element_type=F32)
            for h in range(YN // 2):
                pair = [q[:, (2 * h + a) * 128:(2 * h + a + 1) * 128].reshape(32, 8, 128) for a in range(2)]
                c_ref[v, :, x0 + 16 * h:x0 + 16 * h + 16, :] = jnp.concatenate(pair, axis=1).astype(BF16)

    for k in range(32 // ZM):
        for p in range(2):
            tall = jnp.concatenate([c_ref[2 * p + a, k * ZM:k * ZM + ZM].reshape(ZM * 64, 128) for a in range(2)], axis=1)
            q = jnp.dot(tall, bzt_ref[p], preferred_element_type=F32)
            for a in range(2):
                at = (2 * p + a) * 64
                for y in range(ZM):
                    w = q[y * 64:y * 64 + 64, a * 128:(a + 1) * 128]
                    hi = w.astype(BF16)
                    col = (k * ZM + y) * 128
                    d_ref[at:at + 64, col:col + 128] = hi
                    d_ref[256 + at:256 + at + 64, col:col + 128] = (w - hi.astype(F32)).astype(BF16)

    carry = jnp.zeros((8, 128), F32)
    for k in range(32 // XT):
        p = jnp.dot(bxt_ref[...], d_ref[:, k * XT * 128:(k + 1) * XT * 128], preferred_element_type=F32)
        for y in range(XT):
            f = None
            for v in range(4):
                g = p[v * rows:(v + 1) * rows, y * 128:(y + 1) * 128]
                f = g if f is None else f * g
            carry = finish(k * XT + y, f, carry)
    return carry


def first_kernel(lo_ref, hi_ref, meast_ref, est_ref, kx, bz, bzt, ly, lyt, bxt, new_ref, newb_ref, measx_ref,
                 nat_ref, eb_ref, a_ref, b_ref, c_ref, d_ref):
    for side, ref in enumerate((lo_ref, hi_ref)):
        for v in range(5):
            nat_ref[side, v] = ref[v].astype(F32)

    def turn(y, _):
        col = pl.multiple_of(y * 128, 128)
        for side, near, far, at in ((0, 16, 0, 0), (1, 64, 80, 48)):
            acc = None
            for v in range(4):
                m = nat_ref[side, v, pl.ds(y, 16, stride=32), :]
                acc = m if acc is None else acc + m
                measx_ref[v, y, at:at + 16, :] = m.astype(BF16)
            eb_ref[near:near + 16, pl.ds(col, 128)] = (acc * 0.25).astype(BF16)
            eb_ref[far:far + 16, pl.ds(col, 128)] = nat_ref[side, 4, pl.ds(y, 16, stride=32), :].astype(BF16)
        for v in range(4):
            measx_ref[v, y, 16:48, :] = meast_ref[v, y]
        eb_ref[32:64, pl.ds(col, 128)] = est_ref[y].astype(BF16)
        return 0

    lax.fori_loop(0, 32, turn, 0, unroll=4)

    def finish(y, f, carry):
        e = est_ref[y] * f
        new_ref[y] = e
        newb_ref[y] = e.astype(BF16)
        return carry

    correct(eb_ref, measx_ref, kx, bz, bzt, ly, lyt, bxt, 32, a_ref, b_ref, c_ref, d_ref, finish)


def second_kernel(lo_ref, hi_ref, measx_ref, est_ref, kx, bz, bzt, ly, lyt, bxt, out_ref, ext_ref, sum_ref,
                  eb_ref, a_ref, b_ref, c_ref, d_ref):
    def fill(y, _):
        col = pl.multiple_of(y * 128, 128)
        eb_ref[0:32, pl.ds(col, 128)] = lo_ref[y]
        eb_ref[32:64, pl.ds(col, 128)] = est_ref[y].astype(BF16)
        eb_ref[64:96, pl.ds(col, 128)] = hi_ref[y]
        return 0

    lax.fori_loop(0, 32, fill, 0, unroll=4)

    def finish(y, f, carry):
        mid = est_ref[y] * f[8:40]
        before = lo_ref[y, 16:32, :].astype(F32)[8:16] * f[0:8]
        after = hi_ref[y, 0:16, :].astype(F32)[0:8] * f[40:48]
        out_ref[pl.ds(y, 32, stride=32), :] = mid
        ext_ref[pl.ds(32 + y, 32, stride=32), :] = mid
        ext_ref[pl.ds(y, 1), :] = before[7:8]
        ext_ref[pl.ds(33 * 32 + y, 1), :] = after[0:1]
        return carry + ((mid[0:8] + mid[8:16]) + (mid[16:24] + mid[24:32]))

    total = correct(eb_ref, measx_ref, kx, bz, bzt, ly, lyt, bxt, 48, a_ref, b_ref, c_ref, d_ref, finish)
    sum_ref[...] = jnp.broadcast_to(jnp.sum(total), sum_ref.shape)


SCRATCH = [
    pltpu.VMEM((96, 4096), BF16),
    pltpu.VMEM((256, 4096), BF16),
    pltpu.VMEM((4, 32, 64, 128), F32),
    pltpu.VMEM((4, 32, 64, 128), BF16),
    pltpu.VMEM((512, 4096), BF16),
]
COST = pl.CostEstimate(flops=6 * 10**9, bytes_accessed=8 * 10**6, transcendentals=0)


def first_call(lo, hi, meast, est, mats):
    return pl.pallas_call(
        first_kernel,
        out_shape=[
            jax.ShapeDtypeStruct((32, 32, 128), F32),
            jax.ShapeDtypeStruct((32, 32, 128), BF16),
            jax.ShapeDtypeStruct((4, 32, 64, 128), BF16),
        ],
        in_specs=[VMEM] * 10,
        out_specs=[VMEM] * 3,
        scratch_shapes=[pltpu.VMEM((2, 5, 512, 128), F32)] + SCRATCH,
        compiler_params=pltpu.CompilerParams(vmem_limit_bytes=32 * 2**20),
        cost_estimate=COST,
        name="first_iteration",
    )(lo.reshape(5, 512, 128), hi.reshape(5, 512, 128), meast, est, *mats)


def second_call(lo, hi, measx, est, mats, bricks):
    return pl.pallas_call(
        second_kernel,
        out_shape=[
            jax.ShapeDtypeStruct((1024, 128), F32),
            jax.ShapeDtypeStruct((34 * 32, 128), F32),
            jax.ShapeDtypeStruct((bricks, 1, 128), F32),
        ],
        in_specs=[VMEM] * 10,
        out_specs=[VMEM] * 3,
        scratch_shapes=SCRATCH,
        compiler_params=pltpu.CompilerParams(vmem_limit_bytes=32 * 2**20),
        cost_estimate=COST,
        name="second_iteration",
    )(lo, hi, measx, est, *mats)

YB = 3


def conv_matrix(conv_weight, yb=YB):
    ch = conv_weight.shape[1]
    w = conv_weight.T.reshape(ch, 3, 9 * ch)
    step = 3 * ch
    rows = [jnp.pad(w, ((0, 0), (0, 0), (yo * step, (yb - 1 - yo) * step))) for yo in range(yb)]
    m = jnp.stack(rows, 0)
    return m.transpose(2, 0, 1, 3).reshape(3 * yb * ch, (yb + 2) * step)


def fold_channels(parts):
    sub = lax.broadcasted_iota(jnp.int32, (8, 128), 0)
    for width in (4, 2, 1):
        keep = (sub & width) == 0
        half = len(parts) // 2
        merged = []
        for k in range(half):
            a, b = parts[k], parts[k + half]
            swap = jnp.where(keep, b, a)
            merged.append(jnp.where(keep, a, b) + pltpu.roll(swap, width, 0) if width == 4 else
                          jnp.where(keep, a + pltpu.roll(a, 8 - width, 0), b + pltpu.roll(b, width, 0)))
        parts = merged
    return parts[0]


def conv_kernel(count, tot_ref, flag_ref, est_ref, stem_ref, head_ref, w_ref, out_ref, n_ref, f_ref, *sums):
    planes = est_ref.shape[0] // 32
    ch = stem_ref.shape[1]
    scale = count / jnp.broadcast_to(jnp.sum(tot_ref[...], axis=0), (8, 128))
    lane = lax.broadcasted_iota(jnp.int32, (ch, 128), 1)
    w0, b0 = stem_ref[0], stem_ref[1]
    blank = jnp.zeros((48, planes * 128), jnp.bfloat16)
    for y in (0, 33, 34):
        f_ref[y * 48:(y + 1) * 48, :] = blank

    def plane(e, _):
        at = pl.multiple_of(e * 32, 32)
        col = pl.multiple_of(e * 128, 128)
        v = est_ref[pl.ds(at, 32), :]
        v = (v.reshape(4, 8, 128) * scale[None]).reshape(32, 128)
        n_ref[...] = v
        flag = jnp.where(e == 0, flag_ref[0], jnp.where(e == planes - 1, flag_ref[1], 1.0))
        w, b = w0 * flag, b0 * flag
        for y in range(32):
            row = n_ref[pl.ds(y, ch, stride=0), :]
            f = jnp.maximum(w * row + b, 0.0).astype(jnp.bfloat16)
            at = (y + 1) * 48
            f_ref[at:at + 16, pl.ds(col, 128)] = jnp.where(lane > 0, pltpu.roll(f, 1, 1), jnp.zeros_like(f))
            f_ref[at + 16:at + 32, pl.ds(col, 128)] = f
            f_ref[at + 32:at + 48, pl.ds(col, 128)] = jnp.where(lane < 127, pltpu.roll(f, 127, 1), jnp.zeros_like(f))
        return 0

    lax.fori_loop(0, planes, plane, 0, unroll=17)
    bias = [head_ref[0, 0:8], head_ref[0, 8:16]]
    gain = [head_ref[1, 0:8], head_ref[1, 8:16]]
    m = YB * ch

    for k in range(11):
        p_ref = sums[k % len(sums)]
        at = k * (YB * 48)
        p_ref[...] = jnp.dot(w_ref[...], f_ref[at:at + (YB + 2) * 48, :], preferred_element_type=jnp.float32)
        for yo in range(min(YB, 32 - k * YB)):
            for g in range((planes - 2) // 8):
                parts = []
                for o in range(g * 8, g * 8 + 8):
                    s = None
                    for h in range(2):
                        top = yo * ch + h * 8
                        acc = (p_ref[top:top + 8, o * 128:o * 128 + 128]
                               + p_ref[m + top:m + top + 8, o * 128 + 128:o * 128 + 256]
                               + p_ref[2 * m + top:2 * m + top + 8, o * 128 + 256:o * 128 + 384])
                        acc = jnp.maximum(acc + bias[h], 0.0) * gain[h]
                        s = acc if s is None else s + acc
                    parts.append(s)
                out_ref[pl.ds(g * 256 + k * YB + yo, 8, stride=32), :] = fold_channels(parts)


def conv_call(totals, est, later, count):
    w, stem, head, flags = later
    planes = est.shape[0] // 32
    ch = head.shape[1]
    smem = pl.BlockSpec(memory_space=pltpu.SMEM)
    vmem = pl.BlockSpec(memory_space=pltpu.VMEM)
    return pl.pallas_call(
        functools.partial(conv_kernel, count),
        out_shape=jax.ShapeDtypeStruct(((planes - 2) * 32, 128), jnp.float32),
        in_specs=[vmem, smem, vmem, vmem, vmem, vmem],
        out_specs=vmem,
        scratch_shapes=[
            pltpu.VMEM((32, 128), jnp.float32),
            pltpu.VMEM((35 * 48, planes * 128), jnp.bfloat16),
        ] + [pltpu.VMEM((3 * YB * ch, planes * 128), jnp.float32)],
        compiler_params=pltpu.CompilerParams(vmem_limit_bytes=40 * 2**20),
        cost_estimate=pl.CostEstimate(flops=4 * 10**9, bytes_accessed=2 * 10**6, transcendentals=0),
        name="conv_head",
    )(totals, flags, est, stem, head, w)


def shifted(cells, step):
    count = lax.axis_size("brick")
    pairs = [(i, i + step) for i in range(count) if 0 <= i + step < count]
    return lax.ppermute(cells, "brick", pairs)


def local(measured, psf, stem_params, conv_weight, head_params):
    views, plane_count, row_count, lane_count = measured.shape
    bricks = lax.axis_size("brick")
    up, down = message_call(measured.reshape(views, plane_count * row_count, lane_count))
    lo, hi = shifted(up, 1), shifted(down, -1)
    kernels = psf / jnp.sum(psf, axis=-1, keepdims=True)
    place = lax.axis_index("brick")
    flags = jnp.stack([place > 0, place < bricks - 1]).astype(F32)
    stem = jnp.broadcast_to(stem_params[:, :, None], stem_params.shape + (lane_count,))
    head = jnp.broadcast_to(head_params[:, :, None], head_params.shape + (lane_count,))
    later = (conv_matrix(conv_weight), stem, head, flags)
    *mats, bxt, bxt2, meast, est = prep_call(kernels, measured, later)
    est, estb, measx = first_call(lo, hi, meast, est, mats + [bxt])
    lo, hi = shifted(estb, 1), shifted(estb, -1)
    out, ext, mine = second_call(lo, hi, measx, est, mats + [bxt2], bricks)
    totals = lax.all_to_all(mine, "brick", 0, 0, tiled=True)
    cell_count = bricks * plane_count * row_count * lane_count
    logits = conv_call(totals, ext, later, float(cell_count))
    shape = (plane_count, row_count, lane_count)
    return out.reshape(shape), logits.reshape(shape)


def solution(mesh):
    placed = (P(None, ("span", "brick"), None, None), P(), P(), P(), P())
    return jax.shard_map(
        local,
        mesh=mesh,
        in_specs=placed,
        out_specs=(P(("span", "brick"), None, None), P(("span", "brick"), None, None)),
        check_vma=False,
    )
```

```python
import functools
import jax, jax.numpy as jnp
from jax import lax
from jax.experimental import pallas as pl
from jax.experimental.pallas import tpu as pltpu
from jax.sharding import PartitionSpec as P

F32, BF16 = jnp.float32, jnp.bfloat16
HALO = 16
SMEM = pl.BlockSpec(memory_space=pltpu.SMEM)
VMEM = pl.BlockSpec(memory_space=pltpu.VMEM)


def iotas(shape):
    return lax.broadcasted_iota(jnp.int32, shape, 0), lax.broadcasted_iota(jnp.int32, shape, 1)


def bands(k_ref, dim, index):
    views, taps = k_ref.shape[0], k_ref.shape[2]
    out = [jnp.zeros(index.shape, F32)] * views
    for t in range(taps):
        hit = index == t
        out = [jnp.where(hit, k_ref[v, dim, t], out[v]) for v in range(views)]
    return out


def prep_kernel(k_ref, meas_ref, w_ref, stem_ref, head_ref, flag_ref, kx_ref, bz_ref, bzt_ref, ly_ref, lyt_ref, bxt_ref, bxt2_ref, meast_ref, est_ref, nat_ref):
    views = k_ref.shape[0]
    reach = (k_ref.shape[2] - 1) // 2
    r, c = iotas((64, 96))
    for v, m in enumerate(bands(k_ref, 0, c - r - HALO + reach)):
        kx_ref[v * 64:(v + 1) * 64, :] = m.astype(BF16)
    for ref, rows, first in ((bxt_ref, 32, 0), (bxt2_ref, 48, -8)):
        r, c = iotas((rows, 512))
        for v, m in enumerate(bands(k_ref, 0, (r + first) - ((c & 63) - HALO) + reach)):
            ref[v * rows:(v + 1) * rows, :] = jnp.where(((c >> 6) & 3) == v, m, 0.0).astype(BF16)
    r, c = iotas((128, 128))
    zero = jnp.zeros((128, 128), BF16)
    for ref, sign in ((bz_ref, 1), (bzt_ref, -1)):
        for v, m in enumerate(bands(k_ref, 2, sign * (r - c) + reach)):
            p, a = v // 2, v % 2
            ref[p, a * 128:(a + 1) * 128, a * 128:(a + 1) * 128] = m.astype(BF16)
            ref[p, a * 128:(a + 1) * 128, (1 - a) * 128:(2 - a) * 128] = zero
    r, c = iotas((32, 32))
    er, ec = iotas((256, 32))
    spread = ((er >> 3) == ec).astype(F32).astype(BF16)
    tr, tc = iotas((32, 256))
    spread_t = ((tc >> 3) == tr).astype(F32).astype(BF16)
    fr, fc = iotas((256, 256))
    same = (fr & 7) == (fc & 7)
    for ref, sign in ((ly_ref, 1), (lyt_ref, -1)):
        for v, m in enumerate(bands(k_ref, 1, sign * (c - r) + reach)):
            wide = jnp.dot(spread, m.astype(BF16), preferred_element_type=F32).astype(BF16)
            full = jnp.dot(wide, spread_t, preferred_element_type=F32)
            ref[v] = jnp.where(same, full, 0.0).astype(BF16)
    for v in range(views):
        nat_ref[v] = meas_ref[v].astype(F32)

    def turn(y, _):
        acc = None
        for v in range(views):
            m = nat_ref[v, pl.ds(y, 32, stride=32), :]
            acc = m if acc is None else acc + m
            meast_ref[v, y] = m.astype(BF16)
        est_ref[y] = acc * (1.0 / views)
        return 0

    lax.fori_loop(0, 32, turn, 0)


def prep_call(kernels, measured, later):
    views = measured.shape[0]
    out = [
        ((views * 64, 96), BF16),
        ((2, 256, 256), BF16),
        ((2, 256, 256), BF16),
        ((views, 256, 256), BF16),
        ((views, 256, 256), BF16),
        ((views * 32, 512), BF16),
        ((views * 48, 512), BF16),
        ((views, 32, 32, 128), BF16),
        ((32, 32, 128), F32),
    ]
    return pl.pallas_call(
        prep_kernel,
        out_shape=[jax.ShapeDtypeStruct(s, d) for s, d in out],
        in_specs=[SMEM, VMEM] + [pl.BlockSpec(memory_space=pl.ANY)] * 4,
        out_specs=[VMEM] * len(out),
        scratch_shapes=[pltpu.VMEM((views, 1024, 128), F32)],
        compiler_params=pltpu.CompilerParams(vmem_limit_bytes=16 * 2**20),
        cost_estimate=pl.CostEstimate(flops=10**9, bytes_accessed=20 * 10**6, transcendentals=0),
        name="bands_and_turn",
    )(kernels, measured.reshape(views, 1024, 128), *later)


def message_kernel(meas_ref, up_ref, down_ref):
    views, rows = meas_ref.shape[0], meas_ref.shape[1] // 2
    for ref, near, far in ((up_ref, rows, 0), (down_ref, 0, rows)):
        acc = None
        for v in range(views):
            ref[v] = meas_ref[v, near:near + rows, :]
            m = meas_ref[v, far:far + rows, :].astype(F32)
            acc = m if acc is None else acc + m
        ref[views] = (acc * (1.0 / views)).astype(BF16)


def message_call(measured):
    views, rows, _ = measured.shape
    shape = jax.ShapeDtypeStruct((views + 1, rows // 2, 128), BF16)
    return pl.pallas_call(
        message_kernel,
        out_shape=[shape, shape],
        in_specs=[VMEM],
        out_specs=[VMEM, VMEM],
        compiler_params=pltpu.CompilerParams(vmem_limit_bytes=16 * 2**20),
        name="halo_messages",
    )(measured)


XN, ZM, YN, XT = 8, 8, 2, 8


def correct(eb_ref, meas, kx_ref, bz_ref, bzt_ref, ly_ref, lyt_ref, bxt_ref, rows, a_ref, b_ref, c_ref, d_ref, finish):
    for k in range(32 // XN):
        at = k * XN * 128
        p = jnp.dot(kx_ref[...], eb_ref[:, at:at + XN * 128], preferred_element_type=F32)
        a_ref[:, at:at + XN * 128] = p.astype(BF16)

    for k in range(32 // ZM):
        for p in range(2):
            tall = []
            for y in range(k * ZM, k * ZM + ZM):
                tall.append(jnp.concatenate([a_ref[(2 * p + a) * 64:(2 * p + a) * 64 + 64, y * 128:y * 128 + 128] for a in range(2)], axis=1))
            q = jnp.dot(jnp.concatenate(tall, axis=0), bz_ref[p], preferred_element_type=F32)
            for a in range(2):
                b_ref[2 * p + a, k * ZM:k * ZM + ZM] = q[:, a * 128:(a + 1) * 128].reshape(ZM, 64, 128)

    for v in range(4):
        for k in range(8 // YN):
            x0 = k * YN * 8
            wide = [b_ref[v, :, x0 + 8 * a:x0 + 8 * a + 8, :].reshape(256, 128).astype(BF16) for a in range(YN)]
            q = jnp.dot(ly_ref[v], jnp.concatenate(wide, axis=1), preferred_element_type=F32)
            wide = []
            for h in range(YN // 2):
                m = meas[v, :, x0 + 16 * h:x0 + 16 * h + 16, :].astype(F32)
                for a in range(2):
                    top = m[:, 8 * a:8 * a + 8, :].reshape(256, 128)
                    at = (2 * h + a) * 128
                    low = q[:, at:at + 128]
                    inverse = pl.reciprocal(low, approx=True)
                    ratio = top * (inverse * (2.0 - low * inverse))
                    if not HALO <= x0 + 16 * h < 64 - HALO:
                        ratio = jnp.where(top > 0.0, ratio, 0.0)
                    wide.append(ratio.astype(BF16))
            q = jnp.dot(lyt_ref[v], jnp.concatenate(wide, axis=1), preferred_element_type=F32)
            for h in range(YN // 2):
                pair = [q[:, (2 * h + a) * 128:(2 * h + a + 1) * 128].reshape(32, 8, 128) for a in range(2)]
                c_ref[v, :, x0 + 16 * h:x0 + 16 * h + 16, :] = jnp.concatenate(pair, axis=1).astype(BF16)

    for k in range(32 // ZM):
        for p in range(2):
            tall = jnp.concatenate([c_ref[2 * p + a, k * ZM:k * ZM + ZM].reshape(ZM * 64, 128) for a in range(2)], axis=1)
            q = jnp.dot(tall, bzt_ref[p], preferred_element_type=F32)
            for a in range(2):
                at = (2 * p + a) * 64
                for y in range(ZM):
                    w = q[y * 64:y * 64 + 64, a * 128:(a + 1) * 128]
                    hi = w.astype(BF16)
                    col = (k * ZM + y) * 128
                    d_ref[at:at + 64, col:col + 128] = hi
                    d_ref[256 + at:256 + at + 64, col:col + 128] = (w - hi.astype(F32)).astype(BF16)

    carry = jnp.zeros((8, 128), F32)
    for k in range(32 // XT):
        p = jnp.dot(bxt_ref[...], d_ref[:, k * XT * 128:(k + 1) * XT * 128], preferred_element_type=F32)
        for y in range(XT):
            f = None
            for v in range(4):
                g = p[v * rows:(v + 1) * rows, y * 128:(y + 1) * 128]
                f = g if f is None else f * g
            carry = finish(k * XT + y, f, carry)
    return carry


def first_kernel(lo_ref, hi_ref, meast_ref, est_ref, kx, bz, bzt, ly, lyt, bxt, new_ref, newb_ref, measx_ref,
                 nat_ref, eb_ref, a_ref, b_ref, c_ref, d_ref):
    for side, ref in enumerate((lo_ref, hi_ref)):
        for v in range(5):
            nat_ref[side, v] = ref[v].astype(F32)

    def turn(y, _):
        col = pl.multiple_of(y * 128, 128)
        for side, near, far, at in ((0, 16, 0, 0), (1, 64, 80, 48)):
            acc = None
            for v in range(4):
                m = nat_ref[side, v, pl.ds(y, 16, stride=32), :]
                acc = m if acc is None else acc + m
                measx_ref[v, y, at:at + 16, :] = m.astype(BF16)
            eb_ref[near:near + 16, pl.ds(col, 128)] = (acc * 0.25).astype(BF16)
            eb_ref[far:far + 16, pl.ds(col, 128)] = nat_ref[side, 4, pl.ds(y, 16, stride=32), :].astype(BF16)
        for v in range(4):
            measx_ref[v, y, 16:48, :] = meast_ref[v, y]
        eb_ref[32:64, pl.ds(col, 128)] = est_ref[y].astype(BF16)
        return 0

    lax.fori_loop(0, 32, turn, 0, unroll=4)

    def finish(y, f, carry):
        e = est_ref[y] * f
        new_ref[y] = e
        newb_ref[y] = e.astype(BF16)
        return carry

    correct(eb_ref, measx_ref, kx, bz, bzt, ly, lyt, bxt, 32, a_ref, b_ref, c_ref, d_ref, finish)


def second_kernel(lo_ref, hi_ref, measx_ref, est_ref, kx, bz, bzt, ly, lyt, bxt, ext_ref, sum_ref,
                  eb_ref, a_ref, b_ref, c_ref, d_ref):
    def fill(y, _):
        col = pl.multiple_of(y * 128, 128)
        eb_ref[0:32, pl.ds(col, 128)] = lo_ref[y]
        eb_ref[32:64, pl.ds(col, 128)] = est_ref[y].astype(BF16)
        eb_ref[64:96, pl.ds(col, 128)] = hi_ref[y]
        return 0

    lax.fori_loop(0, 32, fill, 0, unroll=4)

    def finish(y, f, carry):
        mid = est_ref[y] * f[8:40]
        before = lo_ref[y, 16:32, :].astype(F32)[8:16] * f[0:8]
        after = hi_ref[y, 0:16, :].astype(F32)[0:8] * f[40:48]
        ext_ref[pl.ds(32 + y, 32, stride=32), :] = mid
        ext_ref[pl.ds(y, 1), :] = before[7:8]
        ext_ref[pl.ds(33 * 32 + y, 1), :] = after[0:1]
        return carry + ((mid[0:8] + mid[8:16]) + (mid[16:24] + mid[24:32]))

    total = correct(eb_ref, measx_ref, kx, bz, bzt, ly, lyt, bxt, 48, a_ref, b_ref, c_ref, d_ref, finish)
    sum_ref[...] = jnp.broadcast_to(jnp.sum(total), sum_ref.shape)


SCRATCH = [
    pltpu.VMEM((96, 4096), BF16),
    pltpu.VMEM((256, 4096), BF16),
    pltpu.VMEM((4, 32, 64, 128), F32),
    pltpu.VMEM((4, 32, 64, 128), BF16),
    pltpu.VMEM((512, 4096), BF16),
]
COST = pl.CostEstimate(flops=6 * 10**9, bytes_accessed=8 * 10**6, transcendentals=0)


def first_call(lo, hi, meast, est, mats):
    return pl.pallas_call(
        first_kernel,
        out_shape=[
            jax.ShapeDtypeStruct((32, 32, 128), F32),
            jax.ShapeDtypeStruct((32, 32, 128), BF16),
            jax.ShapeDtypeStruct((4, 32, 64, 128), BF16),
        ],
        in_specs=[VMEM] * 10,
        out_specs=[VMEM] * 3,
        scratch_shapes=[pltpu.VMEM((2, 5, 512, 128), F32)] + SCRATCH,
        compiler_params=pltpu.CompilerParams(vmem_limit_bytes=32 * 2**20),
        cost_estimate=COST,
        name="first_iteration",
    )(lo.reshape(5, 512, 128), hi.reshape(5, 512, 128), meast, est, *mats)


def second_call(lo, hi, measx, est, mats, bricks):
    return pl.pallas_call(
        second_kernel,
        out_shape=[
            jax.ShapeDtypeStruct((34 * 32, 128), F32),
            jax.ShapeDtypeStruct((bricks, 1, 128), F32),
        ],
        in_specs=[VMEM] * 10,
        out_specs=[VMEM] * 2,
        scratch_shapes=SCRATCH,
        compiler_params=pltpu.CompilerParams(vmem_limit_bytes=32 * 2**20),
        cost_estimate=COST,
        name="second_iteration",
    )(lo, hi, measx, est, *mats)

YB = 3


def conv_matrix(conv_weight, yb=YB):
    ch = conv_weight.shape[1]
    w = conv_weight.T.reshape(ch, 3, 9 * ch)
    step = 3 * ch
    rows = [jnp.pad(w, ((0, 0), (0, 0), (yo * step, (yb - 1 - yo) * step))) for yo in range(yb)]
    m = jnp.stack(rows, 0)
    return m.transpose(2, 0, 1, 3).reshape(3 * yb * ch, (yb + 2) * step)


def fold_channels(parts):
    sub = lax.broadcasted_iota(jnp.int32, (8, 128), 0)
    for width in (4, 2, 1):
        keep = (sub & width) == 0
        half = len(parts) // 2
        merged = []
        for k in range(half):
            a, b = parts[k], parts[k + half]
            swap = jnp.where(keep, b, a)
            merged.append(jnp.where(keep, a, b) + pltpu.roll(swap, width, 0) if width == 4 else
                          jnp.where(keep, a + pltpu.roll(a, 8 - width, 0), b + pltpu.roll(b, width, 0)))
        parts = merged
    return parts[0]


def conv_kernel(count, tot_ref, flag_ref, est_ref, stem_ref, head_ref, w_ref, out_ref, copy_ref, n_ref, f_ref, sem, *sums):
    planes = est_ref.shape[0] // 32
    ch = stem_ref.shape[1]
    copy = pltpu.make_async_copy(est_ref.at[pl.ds(32, (planes - 2) * 32)], copy_ref, sem)
    copy.start()
    scale = count / jnp.broadcast_to(jnp.sum(tot_ref[...], axis=0), (8, 128))
    lane = lax.broadcasted_iota(jnp.int32, (ch, 128), 1)
    w0, b0 = stem_ref[0], stem_ref[1]
    blank = jnp.zeros((48, planes * 128), jnp.bfloat16)
    for y in (0, 33, 34):
        f_ref[y * 48:(y + 1) * 48, :] = blank

    def plane(e, _):
        at = pl.multiple_of(e * 32, 32)
        col = pl.multiple_of(e * 128, 128)
        v = est_ref[pl.ds(at, 32), :]
        v = (v.reshape(4, 8, 128) * scale[None]).reshape(32, 128)
        n_ref[...] = v
        flag = jnp.where(e == 0, flag_ref[0], jnp.where(e == planes - 1, flag_ref[1], 1.0))
        w, b = w0 * flag, b0 * flag
        for y in range(32):
            row = n_ref[pl.ds(y, ch, stride=0), :]
            f = jnp.maximum(w * row + b, 0.0).astype(jnp.bfloat16)
            at = (y + 1) * 48
            f_ref[at:at + 16, pl.ds(col, 128)] = jnp.where(lane > 0, pltpu.roll(f, 1, 1), jnp.zeros_like(f))
            f_ref[at + 16:at + 32, pl.ds(col, 128)] = f
            f_ref[at + 32:at + 48, pl.ds(col, 128)] = jnp.where(lane < 127, pltpu.roll(f, 127, 1), jnp.zeros_like(f))
        return 0

    lax.fori_loop(0, planes, plane, 0, unroll=17)
    bias = [head_ref[0, 0:8], head_ref[0, 8:16]]
    gain = [head_ref[1, 0:8], head_ref[1, 8:16]]
    m = YB * ch

    for k in range(11):
        p_ref = sums[k % len(sums)]
        at = k * (YB * 48)
        p_ref[...] = jnp.dot(w_ref[...], f_ref[at:at + (YB + 2) * 48, :], preferred_element_type=jnp.float32)
        for yo in range(min(YB, 32 - k * YB)):
            for g in range((planes - 2) // 8):
                parts = []
                for o in range(g * 8, g * 8 + 8):
                    s = None
                    for h in range(2):
                        top = yo * ch + h * 8
                        acc = (p_ref[top:top + 8, o * 128:o * 128 + 128]
                               + p_ref[m + top:m + top + 8, o * 128 + 128:o * 128 + 256]
                               + p_ref[2 * m + top:2 * m + top + 8, o * 128 + 256:o * 128 + 384])
                        acc = jnp.maximum(acc + bias[h], 0.0) * gain[h]
                        s = acc if s is None else s + acc
                    parts.append(s)
                out_ref[pl.ds(g * 256 + k * YB + yo, 8, stride=32), :] = fold_channels(parts)
    copy.wait()


def conv_call(totals, est, later, count):
    w, stem, head, flags = later
    planes = est.shape[0] // 32
    ch = head.shape[1]
    smem = pl.BlockSpec(memory_space=pltpu.SMEM)
    vmem = pl.BlockSpec(memory_space=pltpu.VMEM)
    return pl.pallas_call(
        functools.partial(conv_kernel, count),
        out_shape=[jax.ShapeDtypeStruct(((planes - 2) * 32, 128), jnp.float32)] * 2,
        in_specs=[vmem, smem, vmem, vmem, vmem, vmem],
        out_specs=[vmem, pl.BlockSpec(memory_space=pl.ANY)],
        scratch_shapes=[
            pltpu.VMEM((32, 128), jnp.float32),
            pltpu.VMEM((35 * 48, planes * 128), jnp.bfloat16),
            pltpu.SemaphoreType.DMA(()),
        ] + [pltpu.VMEM((3 * YB * ch, planes * 128), jnp.float32)],
        compiler_params=pltpu.CompilerParams(vmem_limit_bytes=40 * 2**20),
        cost_estimate=pl.CostEstimate(flops=4 * 10**9, bytes_accessed=2 * 10**6, transcendentals=0),
        name="conv_head",
    )(totals, flags, est, stem, head, w)


def shifted(cells, step):
    count = lax.axis_size("brick")
    pairs = [(i, i + step) for i in range(count) if 0 <= i + step < count]
    return lax.ppermute(cells, "brick", pairs)


def local(measured, psf, stem_params, conv_weight, head_params):
    views, plane_count, row_count, lane_count = measured.shape
    bricks = lax.axis_size("brick")
    up, down = message_call(measured.reshape(views, plane_count * row_count, lane_count))
    lo, hi = shifted(up, 1), shifted(down, -1)
    kernels = psf / jnp.sum(psf, axis=-1, keepdims=True)
    place = lax.axis_index("brick")
    flags = jnp.stack([place > 0, place < bricks - 1]).astype(F32)
    stem = jnp.broadcast_to(stem_params[:, :, None], stem_params.shape + (lane_count,))
    head = jnp.broadcast_to(head_params[:, :, None], head_params.shape + (lane_count,))
    later = (conv_matrix(conv_weight), stem, head, flags)
    *mats, bxt, bxt2, meast, est = prep_call(kernels, measured, later)
    est, estb, measx = first_call(lo, hi, meast, est, mats + [bxt])
    lo, hi = shifted(estb, 1), shifted(estb, -1)
    ext, mine = second_call(lo, hi, measx, est, mats + [bxt2], bricks)
    totals = lax.all_to_all(mine, "brick", 0, 0, tiled=True)
    cell_count = bricks * plane_count * row_count * lane_count
    logits, out = conv_call(totals, ext, later, float(cell_count))
    shape = (plane_count, row_count, lane_count)
    return out.reshape(shape), logits.reshape(shape)


def solution(mesh):
    placed = (P(None, ("span", "brick"), None, None), P(), P(), P(), P())
    return jax.shard_map(
        local,
        mesh=mesh,
        in_specs=placed,
        out_specs=(P(("span", "brick"), None, None), P(("span", "brick"), None, None)),
        check_vma=False,
    )
```
